256 devices in a mesh: ctx: 64 (over x, y_hi, z), head: 4 (over y_lo, core).
Axes of the slice: x: 4, y: 4 (y_hi: 2, y_lo: 2; y = y_hi * 2 + y_lo), z: 8, core: 2. Of those that a mesh axis runs over, the one named last changes fastest.
Arguments:
- inputs: bfloat16 [32768, 4096], P('ctx', 'head'), may hold values from -6 to 6
- queries: bfloat16 [32768, 2048], P('ctx', 'head'), may hold values from -25 to 25
- key_rows: bfloat16 [32768, 2048], P('ctx', 'head'), may hold values from -7 to 7
- value_rows: bfloat16 [32768, 2048], P('ctx', 'head'), may hold values from -6 to 6
- output_gradient: bfloat16 [32768, 4096], P('ctx', 'head'), may hold values from -6 to 6
- head_gradients: bfloat16 [32768, 2048], P('ctx', 'head'), may hold values from -6 to 6
- head_shift: int32 [16], P('head'), may hold values from 0 to 1, as said below
- down_qkv: bfloat16 [3, 4096, 16], P(None, 'head'), may hold values from -0.09375 to 0.09375
- up_qkv: bfloat16 [3, 16, 2048], P(None, None, 'head'), may hold values from -0.125 to 0.125
- output_down_adapter: bfloat16 [2048, 16], P('head'), may hold values from -0.125 to 0.125
- up_out: bfloat16 [16, 4096], P(None, 'head'), may hold values from -0.09375 to 0.09375
Outputs:
- projection_gradients: bfloat16 [3, 32768, 2048], P(None, 'ctx', 'head')
- projection_down_gradient: float32 [3, 4096, 16], P(None, 'head')
- projection_up_gradient: float32 [3, 16, 2048], P(None, None, 'head')
- output_down_gradient: float32 [2048, 16], P('head')
- output_up_gradient: float32 [16, 4096], P(None, 'head')
The draws below stay inside these ranges and needn't reach their ends.
Inputs may be any that keep to these rules, and one draw needn't show every extreme that they name: `head_shift`: exactly half of the 16 heads are shifted.
All inputs are finite; a program needn't handle non-finite values.
Results may differ from the reference program's by a relative error of at most 0.015.
Values may be sent and summed in bfloat16 or wider, within the bound.
No kernel may reach another device: no remote copies, remote signals or barrier semaphores. Data moves between devices by JAX's collectives and lax.ppermute only.
A program may use at most 64 MiB of HBM per device.

```python
import jax
import jax.numpy as jnp
from jax import lax

D = 4096
HD = 128
HEADS = 16
R = 16
GROUP = 2048
TOK_DEV = 512
TOKENS = 32768
ATTN_WIDTH = 2048


def drawn_pair(key):
    first, second = jax.random.split(key)
    shape = (TOKENS, HEADS * HD)
    query_part = jnp.clip(jax.random.normal(first, shape, jnp.float32), -4.0, 4.0)
    key_part = jnp.clip(jax.random.normal(second, shape, jnp.float32), -4.0, 4.0)
    return (query_part, key_part)


def draw_queries(key, part):
    result = drawn_pair(key)
    return result[0].astype(jnp.bfloat16)


def draw_key_rows(key, part):
    result = drawn_pair(key)
    return result[1].astype(jnp.bfloat16)


def draw_head_shift(key, part):
    key = jax.random.fold_in(key, 5)
    order = jax.random.permutation(key, HEADS)
    return (order < HEADS // 2).astype(jnp.int32)


def block_scale(own_key, extent, cuts, least, top_value):
    loudness = 1.0
    for axis_at, parts in cuts:
        draws = jax.random.uniform(jax.random.fold_in(jax.random.fold_in(own_key, 6), axis_at), (parts,), jnp.float32, least / len(cuts), top_value / len(cuts))
        loudness = loudness * jnp.repeat(jnp.exp(draws), extent[axis_at] // parts).reshape((-1,) + (1,) * (len(extent) - 1 - axis_at))
    return loudness


def centred(own_key, shape, scale, reach, cuts=(), kind=jnp.bfloat16):
    loudness = block_scale(own_key, shape, cuts, -0.22, 0.18) if cuts else 1.0
    values = jax.random.normal(own_key, shape, jnp.float32) * scale * loudness
    return jnp.minimum(jnp.maximum(values, -reach), reach).astype(kind)


def setup_inputs(seed: int = 0) -> dict:
    arg_keys = jax.random.split(jax.random.key(seed), 12)
    inputs = centred(arg_keys[0], (TOKENS, D), 1.0, 6.0, ((0, 64), (1, 4)))
    queries = draw_queries(jax.random.fold_in(arg_keys[11], 71), 0)
    key_rows = draw_key_rows(jax.random.fold_in(arg_keys[11], 71), 0)
    value_rows = centred(arg_keys[3], (TOKENS, ATTN_WIDTH), 1.0, 6.0, ((0, 64), (1, 4)))
    output_gradient = centred(arg_keys[4], (TOKENS, D), 1.0, 6.0, ((0, 64), (1, 4)))
    head_gradients = centred(arg_keys[5], (TOKENS, ATTN_WIDTH), 1.0, 6.0, ((0, 64), (1, 4)))
    head_shift = draw_head_shift(jax.random.fold_in(arg_keys[11], 71), 0)
    down_qkv = centred(arg_keys[7], (3, D, R), D ** -0.5, 0.09375, ((1, 4),))
    up_qkv = centred(arg_keys[8], (3, R, ATTN_WIDTH), ATTN_WIDTH ** -0.5, 0.125, ((2, 4),))
    output_down_adapter = centred(arg_keys[9], (ATTN_WIDTH, R), ATTN_WIDTH ** -0.5, 0.125, ((0, 4),))
    up_out = centred(arg_keys[10], (R, D), D ** -0.5, 0.09375, ((1, 4),))
    return {"inputs": inputs, "queries": queries, "key_rows": key_rows, "value_rows": value_rows, "output_gradient": output_gradient, "head_gradients": head_gradients, "head_shift": head_shift, "down_qkv": down_qkv, "up_qkv": up_qkv, "output_down_adapter": output_down_adapter, "up_out": up_out}


adapter_scale = 2.0


def grouped(items):
    query_head, key_head, value_head, grad_head = [item.astype(jnp.float32) for item in items]
    factor = HD ** -0.5
    shards = GROUP // TOK_DEV
    row_index = lax.broadcasted_iota(jnp.int32, (GROUP, GROUP), 0)
    col_index = lax.broadcasted_iota(jnp.int32, (GROUP, GROUP), 1)
    visible = col_index <= row_index
    scores = jnp.einsum('td,sd->ts', query_head, key_head) * factor
    scores = jnp.where(visible, scores, -1e30)
    row_peak = jnp.max(scores, axis=1, keepdims=True)
    weights = jnp.where(visible, jnp.exp(scores - row_peak), 0.0)
    attention = weights / jnp.sum(weights, axis=1, keepdims=True)
    attention_bf = attention.astype(jnp.bfloat16)
    frame_out = jnp.einsum('ts,sd->td', attention_bf.astype(jnp.float32), value_head).astype(jnp.bfloat16)
    row_delta = jnp.sum(grad_head * frame_out.astype(jnp.float32), axis=1, keepdims=True)
    dprob = jnp.einsum('td,sd->ts', grad_head, value_head)
    dscore = (attention * (dprob - row_delta)).astype(jnp.bfloat16).astype(jnp.float32)
    grad_query = (jnp.einsum('ts,sd->td', dscore, key_head) * factor).astype(jnp.bfloat16)
    same_shard = jnp.eye(shards, dtype=bool)[:, :, None, None]

    def combine(left, right, scale):
        terms = jnp.einsum('atbs,atd->absd', left.reshape(shards, TOK_DEV, shards, TOK_DEV), right.reshape(shards, TOK_DEV, HD)) * scale
        rounded = lax.optimization_barrier(terms.astype(jnp.bfloat16)).astype(jnp.float32)
        return jnp.sum(jnp.where(same_shard, terms, rounded), axis=0).reshape(GROUP, HD).astype(jnp.bfloat16)

    grad_key = combine(dscore, query_head, factor)
    grad_value = combine(attention_bf.astype(jnp.float32), grad_head, 1.0)
    return grad_query, grad_key, grad_value, frame_out


def reference(inputs, queries, key_rows, value_rows, output_gradient, head_gradients, head_shift, down_qkv, up_qkv, output_down_adapter, up_out):
    half = GROUP // 2
    groups = TOKENS // GROUP
    col_shift = jnp.repeat(head_shift, HD) > 0
    output_rank_product = jnp.einsum('td,rd->tr', output_gradient.astype(jnp.float32), up_out.astype(jnp.float32)).astype(jnp.bfloat16)
    input_lowrank = jnp.einsum('td,kdr->ktr', inputs.astype(jnp.float32), down_qkv.astype(jnp.float32)).astype(jnp.bfloat16)
    attention_gradient = (head_gradients.astype(jnp.float32) + adapter_scale * jnp.einsum('fq,zq->fz', output_rank_product.astype(jnp.float32), output_down_adapter.astype(jnp.float32))).astype(jnp.bfloat16)

    def roll_into(array):
        return jnp.where(col_shift, jnp.roll(array, -half, axis=0), array)

    def roll_out(array):
        return jnp.where(col_shift, jnp.roll(array, half, axis=0), array)

    def split_heads(array):
        return array.reshape(groups, GROUP, HEADS, HD).transpose(0, 2, 1, 3).reshape(groups * HEADS, GROUP, HD)

    def join_heads(array):
        return array.reshape(groups, HEADS, GROUP, HD).transpose(0, 2, 1, 3).reshape(TOKENS, HEADS * HD)

    framed = tuple(split_heads(roll_into(array)) for array in (queries, key_rows, value_rows, attention_gradient))
    results = lax.map(grouped, framed)
    grad_query, grad_key, grad_value, attention_result = [roll_out(join_heads(item)) for item in results]
    projection_gradients = jnp.stack([grad_query, grad_key, grad_value])
    rank_gradient = jnp.einsum('ktc,krc->ktr', projection_gradients.astype(jnp.float32), up_qkv.astype(jnp.float32)).astype(jnp.bfloat16)
    output_lowrank = jnp.einsum('tc,cr->tr', attention_result.astype(jnp.float32), output_down_adapter.astype(jnp.float32)).astype(jnp.bfloat16)
    norm_value = TOKENS ** -0.5
    projection_down_gradient = adapter_scale * jnp.einsum('nj,gnb->gjb', inputs.astype(jnp.float32), rank_gradient.astype(jnp.float32)) * norm_value
    projection_up_gradient = adapter_scale * jnp.einsum('diy,dio->dyo', input_lowrank.astype(jnp.float32), projection_gradients.astype(jnp.float32)) * norm_value
    output_down_gradient = adapter_scale * jnp.einsum('pu,pq->uq', attention_result.astype(jnp.float32), output_rank_product.astype(jnp.float32)) * norm_value
    output_up_gradient = adapter_scale * jnp.einsum('qw,qj->wj', output_lowrank.astype(jnp.float32), output_gradient.astype(jnp.float32)) * norm_value
    return projection_gradients, projection_down_gradient, projection_up_gradient, output_down_gradient, output_up_gradient
```

```python
import functools

import jax
import jax.numpy as jnp
from jax import lax
from jax.experimental import pallas as pl
from jax.experimental.pallas import tpu as pltpu
from jax.sharding import PartitionSpec as P

adapter_scale = 2.0
F32 = jnp.float32
BF16 = jnp.bfloat16
ANY = pl.BlockSpec(memory_space=pl.ANY)
SMEM = pl.BlockSpec(memory_space=pltpu.SMEM)
VMEM = pl.BlockSpec(memory_space=pltpu.VMEM)

ROLE_OF_SLOT = ((3, 0, 2, 1), (0, 1, 3, 2), (1, 2, 0, 3), (2, 3, 1, 0))
SLOT_OF_ROLE = tuple(tuple(row.index(r) for r in range(4)) for row in ROLE_OF_SLOT)


def pick(index, values):
    out = jnp.int32(values[-1]) if isinstance(values[-1], int) else values[-1]
    for i in range(len(values) - 2, -1, -1):
        out = jnp.where(index == i, values[i], out)
    return out


def plan_kernel(shift_ref, me_ref, out_ref):
    place, column = me_ref[0], me_ref[1]
    quarter = lax.rem(place, 4)
    high, core = lax.div(column, 2), lax.rem(column, 2)
    shift = [shift_ref[i] for i in range(16)]
    excess = sum(shift[:8]) - 4
    swaps = jnp.abs(excess)
    low_swaps = lax.div(swaps, 2)
    core_swaps = (low_swaps, swaps - low_swaps)
    first_sends = jnp.where(excess > 0, 1, 0)
    sent_type = jnp.where(high == 0, first_sends, 1 - first_sends)
    other_type = 1 - sent_type
    mine = [jnp.where(high == 0, shift[i], shift[8 + i]) for i in range(8)]
    theirs = [jnp.where(high == 0, shift[8 + i], shift[i]) for i in range(8)]
    rank_sent = jnp.int32(0)
    rank_other = jnp.int32(0)
    kept, worker, role, column_rank = [], [], [], []
    for h in range(8):
        if h % 4 == 0:
            in_column = jnp.int32(0)
        is_sent = mine[h] == sent_type
        keep = jnp.logical_not(is_sent & (in_column < core_swaps[h // 4]))
        column_rank.append(in_column)
        at = jnp.where(is_sent, rank_sent, rank_other)
        room = 2 - core_swaps[0]
        on_core = jnp.where(is_sent, lax.div(at, 2), jnp.where(at < room, 0, 1))
        turn = jnp.where(is_sent, lax.rem(at, 2), jnp.where(at < room, at, at - room))
        kept.append(keep)
        worker.append(on_core)
        role.append(mine[h] * 2 + turn)
        in_column = in_column + jnp.where(is_sent, 1, 0)
        rank_sent = rank_sent + jnp.where(is_sent & keep, 1, 0)
        rank_other = rank_other + jnp.where(is_sent, 0, 1)
    source = [jnp.int32(9), jnp.int32(8), jnp.int32(9), jnp.int32(8)]
    for h in range(8):
        here = jnp.where(core == h // 4, h % 4, 4 + h % 4)
        for r in range(4):
            hit = kept[h] & (worker[h] == core) & (role[h] == r)
            source[r] = jnp.where(hit, here, source[r])
    slots = [pick(quarter, [ROLE_OF_SLOT[j][s] for j in range(4)]) for s in range(4)]
    for s in range(4):
        out_ref[s] = pick(slots[s], source)
    slot_of = [pick(quarter, [SLOT_OF_ROLE[j][r] for j in range(4)]) for r in range(4)]
    for want in range(2):
        out_index = jnp.int32(0)
        in_index = jnp.int32(0)
        seen = jnp.int32(0)
        for i in range(4):
            own = jnp.where(core == 0, mine[i], mine[4 + i])
            rank = jnp.where(core == 0, column_rank[i], column_rank[4 + i])
            out_index = jnp.where((own == sent_type) & (rank == want), i, out_index)
            far = jnp.where(core == 0, theirs[i], theirs[4 + i])
            in_index = jnp.where((far == other_type) & (seen == want), i, in_index)
            seen = seen + jnp.where(far == other_type, 1, 0)
        out_ref[4 + want] = out_index
        out_ref[14 + want] = in_index
    out_ref[6] = pick(other_type * 2 + 1, slot_of)
    out_ref[7] = pick(other_type * 2, slot_of)
    for i in range(4):
        keep = jnp.where(core == 0, kept[i], kept[4 + i])
        on_core = jnp.where(core == 0, worker[i], worker[4 + i])
        rank = jnp.where(core == 0, column_rank[i], column_rank[4 + i])
        which = jnp.where(core == 0, role[i], role[4 + i])
        back = pick(which, slot_of) + jnp.where(on_core == core, 0, 4)
        out_ref[8 + i] = jnp.where(keep, back, 8 + rank)
    out_ref[12] = jnp.minimum(swaps, 3)
    found = pick(slots[0], source)
    near = lax.rem(found, 4)
    out_ref[13] = jnp.where(
        found < 4,
        column * 4 + near,
        jnp.where(
            found < 8,
            (column + 1 - 2 * core) * 4 + near,
            (column + 2 - 4 * high) * 4 + jnp.where(found == 8, out_ref[14], out_ref[15]),
        ),
    )


def make_plan(shift_all, place, column):
    return pl.pallas_call(
        plan_kernel,
        out_shape=jax.ShapeDtypeStruct((16,), jnp.int32),
        in_specs=[SMEM, SMEM],
        out_specs=SMEM,
        name="plan",
    )(shift_all, jnp.stack([place, column]).astype(jnp.int32))


def column_of(ref, index, width):
    return ref.at[:, pl.ds(pl.multiple_of(index * width, width), width)]


def far_pack(plan, arrays, width):
    count = len(arrays)
    rows = arrays[0].shape[0]

    def body(plan_ref, *refs):
        own, out, sems = refs[:count], refs[count], refs[count + 1]
        copies = []
        for r in range(2):
            for t in range(count):
                copy = pltpu.make_async_copy(
                    column_of(own[t], plan_ref[4 + r], width), out.at[r, t], sems.at[r, t]
                )
                copy.start()
                copies.append(copy)
        for copy in copies:
            copy.wait()

    return pl.pallas_call(
        body,
        out_shape=jax.ShapeDtypeStruct((2, count, rows, width), arrays[0].dtype),
        in_specs=[SMEM] + [ANY] * count,
        out_specs=ANY,
        scratch_shapes=[pltpu.SemaphoreType.DMA((2, count))],
        name="far_pack",
    )(plan, *arrays)


def slot_pack(plan, own_arrays, sibling_arrays, far, width):
    count = len(own_arrays)
    rows = own_arrays[0].shape[0]

    def body(plan_ref, *refs):
        own, sib = refs[:count], refs[count : 2 * count]
        far_ref = refs[2 * count]
        outs = refs[2 * count + 1 : 2 * count + 5]
        sems = refs[2 * count + 5]
        for s in range(4):
            source = plan_ref[s]

            @pl.when(source < 4)
            def _(s=s, source=source):
                for t in range(count):
                    pltpu.make_async_copy(
                        column_of(own[t], source, width), outs[s].at[t], sems.at[s, t]
                    ).start()

            @pl.when((source >= 4) & (source < 8))
            def _(s=s, source=source):
                for t in range(count):
                    pltpu.make_async_copy(
                        column_of(sib[t], source - 4, width), outs[s].at[t], sems.at[s, t]
                    ).start()

            @pl.when(source >= 8)
            def _(s=s, source=source):
                for t in range(count):
                    pltpu.make_async_copy(
                        far_ref.at[source - 8, t], outs[s].at[t], sems.at[s, t]
                    ).start()

        for s in range(4):
            for t in range(count):
                pltpu.make_async_copy(far_ref.at[0, t], outs[s].at[t], sems.at[s, t]).wait()

    return pl.pallas_call(
        body,
        out_shape=[jax.ShapeDtypeStruct((count, rows, width), own_arrays[0].dtype)] * 4,
        in_specs=[SMEM] + [ANY] * (2 * count + 1),
        out_specs=[ANY] * 4,
        scratch_shapes=[pltpu.SemaphoreType.DMA((4, count))],
        name="slot_pack",
    )(plan, *own_arrays, *sibling_arrays, far)


def far_return_pack(plan, slots):
    count, rows, width = slots[0].shape

    def body(plan_ref, *refs):
        ins, out, sems = refs[:4], refs[4], refs[5]
        for r in range(2):
            for s in range(4):

                @pl.when(plan_ref[6 + r] == s)
                def _(r=r, s=s):
                    pltpu.make_async_copy(ins[s], out.at[r], sems.at[r]).start()

        for r in range(2):
            pltpu.make_async_copy(ins[0], out.at[r], sems.at[r]).wait()

    return pl.pallas_call(
        body,
        out_shape=jax.ShapeDtypeStruct((2, count, rows, width), slots[0].dtype),
        in_specs=[SMEM] + [ANY] * 4,
        out_specs=ANY,
        scratch_shapes=[pltpu.SemaphoreType.DMA((2,))],
        name="far_return_pack",
    )(plan, *slots)


def head_unpack(plan, own_slots, sibling_slots, far, heads):
    count, rows, width = own_slots[0].shape

    def body(plan_ref, *refs):
        own, sib, far_ref = refs[:4], refs[4:8], refs[8]
        grads, attn, sems = refs[9], refs[10], refs[11]

        def target(t, i):
            columns = pl.ds(i * width, width)
            return grads.at[t, :, columns] if t < 3 else attn.at[:, columns]

        for i in range(heads):
            source = plan_ref[8 + i]
            for s in range(10):
                place = own[s] if s < 4 else sib[s - 4] if s < 8 else far_ref.at[s - 8]

                @pl.when(source == s)
                def _(i=i, place=place):
                    for t in range(count):
                        pltpu.make_async_copy(place.at[t], target(t, i), sems.at[i, t]).start()

        for i in range(heads):
            for t in range(count):
                pltpu.make_async_copy(own[0].at[t], target(t, i), sems.at[i, t]).wait()

    return pl.pallas_call(
        body,
        out_shape=[
            jax.ShapeDtypeStruct((3, rows, heads * width), own_slots[0].dtype),
            jax.ShapeDtypeStruct((rows, heads * width), own_slots[0].dtype),
        ],
        in_specs=[SMEM] + [ANY] * 9,
        out_specs=[ANY] * 2,
        scratch_shapes=[pltpu.SemaphoreType.DMA((heads, count))],
        name="head_unpack",
    )(plan, *own_slots, *sibling_slots, far)


def dot_nt(a, b):
    return lax.dot_general(a, b, (((1,), (1,)), ((), ())), preferred_element_type=F32)


def dot_nn(a, b):
    return lax.dot_general(a, b, (((1,), (0,)), ((), ())), preferred_element_type=F32)


def dot_tn(a, b):
    return lax.dot_general(a, b, (((0,), (0,)), ((), ())), preferred_element_type=F32)


def attend_body(
    block, plan_ref, me_ref, left, own, right, far, rank_l, rank_o, rank_r, rank_f, down,
    out_l, out_o, out_r, out_f,
    grad_rows, held, made, ranks, down_held, key_sum, value_sum, in_sems, rank_sems, out_sems,
):
    del grad_rows
    rows, width = own.shape[1], own.shape[2]
    total = 4 * rows
    factor = width**-0.5
    odd = lax.rem(me_ref[0], 2)
    starts = [(1 - odd) * rows, (2 - odd) * rows, (3 - odd) * rows, odd * 3 * rows]

    def at(i):
        return pl.ds(pl.multiple_of(starts[i], rows), rows)

    copies = []
    for i, source in enumerate((left, own, right, far)):
        copy = pltpu.make_async_copy(source, held.at[:, at(i)], in_sems.at[i])
        copy.start()
        copies.append(copy)
    for i, source in enumerate((rank_l, rank_o, rank_r, rank_f)):
        copy = pltpu.make_async_copy(source, ranks.at[at(i)], rank_sems.at[i])
        copy.start()
        copies.append(copy)
    copy = pltpu.make_async_copy(
        down.at[pl.ds(pl.multiple_of(plan_ref[13] * width, width), width)],
        down_held,
        rank_sems.at[4],
    )
    copy.start()
    copies.append(copy)
    key_sum[...] = jnp.zeros_like(key_sum)
    value_sum[...] = jnp.zeros_like(value_sum)
    for copy in copies:
        copy.wait()
    held[3] = (
        held[3].astype(F32) + adapter_scale * dot_nt(ranks[...], down_held[...])
    ).astype(BF16)
    mask = lax.broadcasted_iota(jnp.int32, (block, block), 1) <= lax.broadcasted_iota(
        jnp.int32, (block, block), 0
    )
    for i in reversed(range(total // block)):
        here = pl.ds(i * block, block)
        span = (i + 1) * block
        query, grad = held[0, here, :], held[3, here, :]
        keys, values = held[1, :span, :], held[2, :span, :]
        score = dot_nt(query, keys) * (factor * 1.4426950408889634)
        last = jnp.where(mask, score[:, i * block :], -1e30)
        score = jnp.concatenate([score[:, : i * block], last], axis=1) if i else last
        peak = jnp.max(score, axis=1, keepdims=True)
        weight = jnp.exp2(score - peak)
        attention = weight * (1.0 / jnp.sum(weight, axis=1, keepdims=True))
        attention_bf = attention.astype(BF16)
        out = dot_nn(attention_bf, values).astype(BF16)
        delta = jnp.sum(grad.astype(F32) * out.astype(F32), axis=1, keepdims=True)
        dscore = (attention * (dot_nt(grad, values) - delta)).astype(BF16)
        made[0, here, :] = (dot_nn(dscore, keys) * factor).astype(BF16)
        made[3, here, :] = out
        key_sum[:span, :] += dot_tn(dscore, query)
        value_sum[:span, :] += dot_tn(attention_bf, grad)
    made[1] = (key_sum[...] * factor).astype(BF16)
    made[2] = value_sum[...].astype(BF16)
    copies = []
    for i, target in enumerate((out_l, out_o, out_r, out_f)):
        copy = pltpu.make_async_copy(made.at[:, at(i)], target, out_sems.at[i])
        copy.start()
        copies.append(copy)
    for copy in copies:
        copy.wait()


def attend(plan, me, units, ranks, down, block=256):
    count, rows, width = units[0].shape
    total = 4 * rows
    rank = ranks[0].shape[1]
    return pl.pallas_call(
        functools.partial(attend_body, min(block, rows)),
        out_shape=[jax.ShapeDtypeStruct((4, rows, width), BF16)] * 4,
        in_specs=[SMEM, SMEM] + [ANY] * 9,
        out_specs=[ANY] * 4,
        scratch_shapes=[
            pltpu.VMEM((8, 128), F32),
            pltpu.VMEM((4, total, width), BF16),
            pltpu.VMEM((4, total, width), BF16),
            pltpu.VMEM((total, rank), BF16),
            pltpu.VMEM((width, rank), BF16),
            pltpu.VMEM((total, width), F32),
            pltpu.VMEM((total, width), F32),
            pltpu.SemaphoreType.DMA((4,)),
            pltpu.SemaphoreType.DMA((5,)),
            pltpu.SemaphoreType.DMA((4,)),
        ],
        compiler_params=pltpu.CompilerParams(vmem_limit_bytes=56 * 2**20),
        name="attend",
    )(plan, me, *units, *ranks, down)


def move(x, axis, target):
    count = lax.axis_size(axis)
    return lax.ppermute(x, axis, [(i, target(i) % count) for i in range(count)])


def up(x):
    return move(x, "ctx", lambda i: i + 1)


def down_one(x):
    return move(x, "ctx", lambda i: i - 1)


def cross(x):
    return move(x, "ctx", lambda i: i + 2 if i % 2 == 0 else i - 2)


def cross_back(x):
    return move(x, "ctx", lambda i: i - 2 if i % 2 == 0 else i + 2)


def sibling(x):
    return move(x, "head", lambda i: i ^ 1)


def far_exchange(case, x):
    def none(x):
        return x

    def one(x):
        return x.at[0].set(lax.ppermute(x[0], "head", [(1, 3), (3, 1)]))

    def two(x):
        return x.at[0].set(move(x[0], "head", lambda i: i ^ 2))

    def more(x):
        return move(x, "head", lambda i: i ^ 2)

    return lax.switch(case, (none, one, two, more), x)


def shards(
    inputs,
    queries,
    key_rows,
    value_rows,
    output_gradient,
    head_gradients,
    head_shift,
    down_qkv,
    up_qkv,
    output_down_adapter,
    up_out,
):
    rows_here, width = queries.shape
    heads_here = head_shift.shape[0]
    head_dim = width // heads_here
    place = lax.axis_index("ctx")
    column = lax.axis_index("head")
    me = jnp.stack([place, column]).astype(jnp.int32)
    shift_all = lax.all_gather(head_shift, "head", tiled=True)
    plan = make_plan(shift_all, place, column)
    case = plan[12]

    own = (queries, key_rows, value_rows, head_gradients)
    with jax.named_scope("heads_in"):
        sib = tuple(sibling(x) for x in own)
        far = far_exchange(case, far_pack(plan, own, head_dim))
        slots = slot_pack(plan, own, sib, far, head_dim)
        units = (up(slots[1]), slots[0], down_one(slots[2]), cross(slots[3]))

    with jax.named_scope("ranks_in"):
        output_part = jnp.einsum(
            "td,rd->tr", output_gradient, up_out, preferred_element_type=F32
        )
        input_part = jnp.einsum("td,kdr->ktr", inputs, down_qkv, preferred_element_type=F32)
        input_sum, output_sum = lax.psum((input_part, output_part), "head")
        input_lowrank = input_sum.astype(BF16)
        output_rank = output_sum.astype(BF16)
        ranks = (up(output_rank), output_rank, down_one(output_rank), cross(output_rank))
        down_all = lax.all_gather(output_down_adapter, "head", tiled=True)

    results = attend(plan, me, units, ranks, down_all)

    with jax.named_scope("heads_back"):
        back = (
            results[1],
            down_one(results[0]),
            up(results[2]),
            cross_back(results[3]),
        )
        back_sib = tuple(sibling(x) for x in back)
        back_far = far_exchange(case, far_return_pack(plan, back))
        projection_gradients, attention_result = head_unpack(
            plan, back, back_sib, back_far, heads_here
        )

    with jax.named_scope("adapters"):
        grad_part = jnp.einsum(
            "ktc,krc->ktr", projection_gradients, up_qkv, preferred_element_type=F32
        )
        out_part = jnp.einsum(
            "tc,cr->tr", attention_result, output_down_adapter, preferred_element_type=F32
        )
        grad_sum, out_sum = lax.psum((grad_part, out_part), "head")
        rank_gradient = grad_sum.astype(BF16)
        output_lowrank = out_sum.astype(BF16)
        projection_down = jnp.einsum(
            "nj,gnb->gjb", inputs, rank_gradient, preferred_element_type=F32
        )
        projection_up = jnp.einsum(
            "diy,dio->dyo", input_lowrank, projection_gradients, preferred_element_type=F32
        )
        output_down = jnp.einsum(
            "pu,pq->uq", attention_result, output_rank, preferred_element_type=F32
        )
        output_up = jnp.einsum(
            "qw,qj->wj", output_lowrank, output_gradient, preferred_element_type=F32
        )
        summed = lax.psum((projection_down, projection_up, output_down, output_up), "ctx")
        scale = adapter_scale * (rows_here * lax.axis_size("ctx")) ** (-0.5)
    return (projection_gradients, *(x * scale for x in summed))


def solution(mesh):
    placed = (
        P("ctx", "head"),
        P("ctx", "head"),
        P("ctx", "head"),
        P("ctx", "head"),
        P("ctx", "head"),
        P("ctx", "head"),
        P("head"),
        P(None, "head", None),
        P(None, None, "head"),
        P("head", None),
        P(None, "head"),
    )
    return jax.shard_map(
        shards,
        mesh=mesh,
        in_specs=placed,
        out_specs=(
            P(None, "ctx", "head"),
            P(None, "head", None),
            P(None, None, "head"),
            P("head", None),
            P(None, "head"),
        ),
        check_vma=False,
    )
```

```python
import functools

import jax
import jax.numpy as jnp
from jax import lax
from jax.experimental import pallas as pl
from jax.experimental.pallas import tpu as pltpu
from jax.sharding import PartitionSpec as P

adapter_scale = 2.0
F32 = jnp.float32
BF16 = jnp.bfloat16
ANY = pl.BlockSpec(memory_space=pl.ANY)
SMEM = pl.BlockSpec(memory_space=pltpu.SMEM)
VMEM = pl.BlockSpec(memory_space=pltpu.VMEM)
PARAMS = pltpu.CompilerParams(vmem_limit_bytes=40 * 2**20)

ROLE_OF_SLOT = ((3, 0, 2, 1), (0, 1, 3, 2), (1, 2, 0, 3), (2, 3, 1, 0))
SLOT_OF_ROLE = tuple(tuple(row.index(r) for r in range(4)) for row in ROLE_OF_SLOT)


def pick(index, values):
    out = jnp.int32(values[-1]) if isinstance(values[-1], int) else values[-1]
    for i in range(len(values) - 2, -1, -1):
        out = jnp.where(index == i, values[i], out)
    return out


def plan_kernel(own_ref, sib_ref, far_ref, cross_ref, me_ref, out_ref, case_ref):
    place, column = me_ref[0], me_ref[1]
    quarter = lax.rem(place, 4)
    high, core = lax.div(column, 2), lax.rem(column, 2)

    def chip(near, other):
        first = [jnp.where(core == 0, near[i], other[i]) for i in range(4)]
        second = [jnp.where(core == 0, other[i], near[i]) for i in range(4)]
        return first + second

    mine, theirs = chip(own_ref, sib_ref), chip(far_ref, cross_ref)
    excess = sum(mine) - 4
    swaps = jnp.abs(excess)
    low_swaps = lax.div(swaps, 2)
    core_swaps = (low_swaps, swaps - low_swaps)
    sent_type = jnp.where(excess > 0, 1, jnp.where(excess < 0, 0, 1 - high))
    other_type = 1 - sent_type
    rank_sent = jnp.int32(0)
    rank_other = jnp.int32(0)
    kept, worker, role, column_rank = [], [], [], []
    for h in range(8):
        if h % 4 == 0:
            in_column = jnp.int32(0)
        is_sent = mine[h] == sent_type
        keep = jnp.logical_not(is_sent & (in_column < core_swaps[h // 4]))
        column_rank.append(in_column)
        at = jnp.where(is_sent, rank_sent, rank_other)
        room = 2 - core_swaps[0]
        on_core = jnp.where(is_sent, lax.div(at, 2), jnp.where(at < room, 0, 1))
        turn = jnp.where(is_sent, lax.rem(at, 2), jnp.where(at < room, at, at - room))
        kept.append(keep)
        worker.append(on_core)
        role.append(mine[h] * 2 + turn)
        in_column = in_column + jnp.where(is_sent, 1, 0)
        rank_sent = rank_sent + jnp.where(is_sent & keep, 1, 0)
        rank_other = rank_other + jnp.where(is_sent, 0, 1)
    source = [jnp.int32(9), jnp.int32(8), jnp.int32(9), jnp.int32(8)]
    for h in range(8):
        here = jnp.where(core == h // 4, h % 4, 4 + h % 4)
        for r in range(4):
            hit = kept[h] & (worker[h] == core) & (role[h] == r)
            source[r] = jnp.where(hit, here, source[r])
    slots = [pick(quarter, [ROLE_OF_SLOT[j][s] for j in range(4)]) for s in range(4)]
    for s in range(4):
        out_ref[s] = pick(slots[s], source)
    slot_of = [pick(quarter, [SLOT_OF_ROLE[j][r] for j in range(4)]) for r in range(4)]
    for want in range(2):
        out_index = jnp.int32(0)
        in_index = jnp.int32(0)
        seen = jnp.int32(0)
        for i in range(4):
            own = jnp.where(core == 0, mine[i], mine[4 + i])
            rank = jnp.where(core == 0, column_rank[i], column_rank[4 + i])
            out_index = jnp.where((own == sent_type) & (rank == want), i, out_index)
            far = jnp.where(core == 0, theirs[i], theirs[4 + i])
            in_index = jnp.where((far == other_type) & (seen == want), i, in_index)
            seen = seen + jnp.where(far == other_type, 1, 0)
        out_ref[4 + want] = out_index
        out_ref[14 + want] = in_index
    out_ref[6] = pick(other_type * 2 + 1, slot_of)
    out_ref[7] = pick(other_type * 2, slot_of)
    for i in range(4):
        keep = jnp.where(core == 0, kept[i], kept[4 + i])
        on_core = jnp.where(core == 0, worker[i], worker[4 + i])
        rank = jnp.where(core == 0, column_rank[i], column_rank[4 + i])
        which = jnp.where(core == 0, role[i], role[4 + i])
        back = pick(which, slot_of) + jnp.where(on_core == core, 0, 4)
        out_ref[8 + i] = jnp.where(keep, back, 8 + rank)
    case_ref[0] = jnp.minimum(swaps, 3)
    found = pick(slots[0], source)
    near = lax.rem(found, 4)
    out_ref[13] = jnp.where(
        found < 4,
        column * 4 + near,
        jnp.where(
            found < 8,
            (column + 1 - 2 * core) * 4 + near,
            (column + 2 - 4 * high) * 4 + jnp.where(found == 8, out_ref[14], out_ref[15]),
        ),
    )


def make_plan(shift, me):
    return pl.pallas_call(
        plan_kernel,
        out_shape=[jax.ShapeDtypeStruct((16,), jnp.int32), jax.ShapeDtypeStruct((1,), jnp.int32)],
        in_specs=[SMEM] * 5,
        out_specs=[SMEM] * 2,
        name="plan",
    )(shift, *(move(shift, "head", lambda i, k=k: i ^ k) for k in (1, 2, 3)), me)


def column_of(ref, index, width):
    return ref.at[:, pl.ds(pl.multiple_of(index * width, width), width)]


def far_pack(plan, arrays, width):
    count = len(arrays)
    rows = arrays[0].shape[0]

    def body(plan_ref, *refs):
        own, out, sems = refs[:count], refs[count], refs[count + 1]
        copies = []
        for r in range(2):
            for t in range(count):
                copy = pltpu.make_async_copy(
                    column_of(own[t], plan_ref[4 + r], width), out.at[r, t], sems.at[r, t]
                )
                copy.start()
                copies.append(copy)
        for copy in copies:
            copy.wait()

    return pl.pallas_call(
        body,
        out_shape=jax.ShapeDtypeStruct((2, count, rows, width), arrays[0].dtype),
        in_specs=[SMEM] + [ANY] * count,
        out_specs=VMEM,
        scratch_shapes=[pltpu.SemaphoreType.DMA((2, count))],
        compiler_params=PARAMS,
        name="far_pack",
    )(plan, *arrays)


def slot_pack(plan, own_arrays, sibling_arrays, far, width):
    count = len(own_arrays)
    rows = own_arrays[0].shape[0]

    def body(plan_ref, *refs):
        own, sib = refs[:count], refs[count : 2 * count]
        far_ref = refs[2 * count]
        outs = refs[2 * count + 1 : 2 * count + 5]
        sems = refs[2 * count + 5]
        for s in range(4):
            source = plan_ref[s]

            @pl.when(source < 4)
            def _(s=s, source=source):
                for t in range(count):
                    pltpu.make_async_copy(
                        column_of(own[t], source, width), outs[s].at[t], sems.at[s, t]
                    ).start()

            @pl.when((source >= 4) & (source < 8))
            def _(s=s, source=source):
                for t in range(count):
                    pltpu.make_async_copy(
                        column_of(sib[t], source - 4, width), outs[s].at[t], sems.at[s, t]
                    ).start()

            @pl.when(source >= 8)
            def _(s=s, source=source):
                for t in range(count):
                    pltpu.make_async_copy(
                        far_ref.at[source - 8, t], outs[s].at[t], sems.at[s, t]
                    ).start()

        for s in range(4):
            for t in range(count):
                pltpu.make_async_copy(far_ref.at[0, t], outs[s].at[t], sems.at[s, t]).wait()

    return pl.pallas_call(
        body,
        out_shape=[jax.ShapeDtypeStruct((count, rows, width), own_arrays[0].dtype)] * 4,
        in_specs=[SMEM] + [ANY] * (2 * count + 1),
        out_specs=[VMEM] * 4,
        scratch_shapes=[pltpu.SemaphoreType.DMA((4, count))],
        compiler_params=PARAMS,
        name="slot_pack",
    )(plan, *own_arrays, *sibling_arrays, far)


def far_return_pack(plan, slots):
    count, rows, width = slots[0].shape

    def body(plan_ref, *refs):
        ins, out, sems = refs[:4], refs[4], refs[5]
        for r in range(2):
            for s in range(4):

                @pl.when(plan_ref[6 + r] == s)
                def _(r=r, s=s):
                    pltpu.make_async_copy(ins[s], out.at[r], sems.at[r]).start()

        for r in range(2):
            pltpu.make_async_copy(ins[0], out.at[r], sems.at[r]).wait()

    return pl.pallas_call(
        body,
        out_shape=jax.ShapeDtypeStruct((2, count, rows, width), slots[0].dtype),
        in_specs=[SMEM] + [ANY] * 4,
        out_specs=VMEM,
        scratch_shapes=[pltpu.SemaphoreType.DMA((2,))],
        compiler_params=PARAMS,
        name="far_return_pack",
    )(plan, *slots)


def head_unpack(plan, own_slots, sibling_slots, far, heads):
    count, rows, width = own_slots[0].shape

    def body(plan_ref, *refs):
        own, sib, far_ref = refs[:4], refs[4:8], refs[8]
        grads, attn, sems = refs[9], refs[10], refs[11]

        def target(t, i):
            columns = pl.ds(i * width, width)
            return grads.at[t, :, columns] if t < 3 else attn.at[:, columns]

        for i in range(heads):
            source = plan_ref[8 + i]
            for s in range(10):
                place = own[s] if s < 4 else sib[s - 4] if s < 8 else far_ref.at[s - 8]

                @pl.when(source == s)
                def _(i=i, place=place):
                    for t in range(count):
                        pltpu.make_async_copy(place.at[t], target(t, i), sems.at[i, t]).start()

        for i in range(heads):
            for t in range(count):
                pltpu.make_async_copy(own[0].at[t], target(t, i), sems.at[i, t]).wait()

    return pl.pallas_call(
        body,
        out_shape=[
            jax.ShapeDtypeStruct((3, rows, heads * width), own_slots[0].dtype),
            jax.ShapeDtypeStruct((rows, heads * width), own_slots[0].dtype),
        ],
        in_specs=[SMEM] + [ANY] * 9,
        out_specs=[VMEM] * 2,
        scratch_shapes=[pltpu.SemaphoreType.DMA((heads, count))],
        compiler_params=PARAMS,
        name="head_unpack",
    )(plan, *own_slots, *sibling_slots, far)


def dot_nt(a, b):
    return lax.dot_general(a, b, (((1,), (1,)), ((), ())), preferred_element_type=F32)


def dot_nn(a, b):
    return lax.dot_general(a, b, (((1,), (0,)), ((), ())), preferred_element_type=F32)


def dot_tn(a, b):
    return lax.dot_general(a, b, (((0,), (0,)), ((), ())), preferred_element_type=F32)


def attend_body(
    block, plan_ref, me_ref, left, own, right, far, rank_l, rank_o, rank_r, rank_f, down,
    out_l, out_o, out_r, out_f,
    held, made, ranks, down_held, key_sum, value_sum, in_sems, rank_sems, out_sems,
):
    rows, width = own.shape[1], own.shape[2]
    total = 4 * rows
    factor = width**-0.5
    odd = lax.rem(me_ref[0], 2)
    starts = [(1 - odd) * rows, (2 - odd) * rows, (3 - odd) * rows, odd * 3 * rows]

    def at(i):
        return pl.ds(pl.multiple_of(starts[i], rows), rows)

    copies = []
    for i, source in enumerate((left, own, right, far)):
        copy = pltpu.make_async_copy(source, held.at[:, at(i)], in_sems.at[i])
        copy.start()
        copies.append(copy)
    for i, source in enumerate((rank_l, rank_o, rank_r, rank_f)):
        copy = pltpu.make_async_copy(source, ranks.at[at(i)], rank_sems.at[i])
        copy.start()
        copies.append(copy)
    copy = pltpu.make_async_copy(
        down.at[pl.ds(pl.multiple_of(plan_ref[13] * width, width), width)],
        down_held,
        rank_sems.at[4],
    )
    copy.start()
    copies.append(copy)
    key_sum[...] = jnp.zeros_like(key_sum)
    value_sum[...] = jnp.zeros_like(value_sum)
    for copy in copies:
        copy.wait()
    held[3] = (
        held[3].astype(F32) + adapter_scale * dot_nt(ranks[...], down_held[...])
    ).astype(BF16)
    mask = lax.broadcasted_iota(jnp.int32, (block, block), 1) <= lax.broadcasted_iota(
        jnp.int32, (block, block), 0
    )
    for i in reversed(range(total // block)):
        here = pl.ds(i * block, block)
        span = (i + 1) * block
        query, grad = held[0, here, :], held[3, here, :]
        keys, values = held[1, :span, :], held[2, :span, :]
        score = dot_nt(query, keys) * (factor * 1.4426950408889634)
        last = jnp.where(mask, score[:, i * block :], -1e30)
        score = jnp.concatenate([score[:, : i * block], last], axis=1) if i else last
        peak = jnp.max(score, axis=1, keepdims=True)
        weight = jnp.exp2(score - peak)
        attention = weight * (1.0 / jnp.sum(weight, axis=1, keepdims=True))
        attention_bf = attention.astype(BF16)
        out = dot_nn(attention_bf, values).astype(BF16)
        delta = jnp.sum(grad.astype(F32) * out.astype(F32), axis=1, keepdims=True)
        dscore = (attention * (dot_nt(grad, values) - delta)).astype(BF16)
        made[0, here, :] = (dot_nn(dscore, keys) * factor).astype(BF16)
        made[3, here, :] = out
        key_sum[:span, :] += dot_tn(dscore, query)
        value_sum[:span, :] += dot_tn(attention_bf, grad)
    made[1] = (key_sum[...] * factor).astype(BF16)
    made[2] = value_sum[...].astype(BF16)
    copies = []
    for i, target in enumerate((out_l, out_o, out_r, out_f)):
        copy = pltpu.make_async_copy(made.at[:, at(i)], target, out_sems.at[i])
        copy.start()
        copies.append(copy)
    for copy in copies:
        copy.wait()


def attend(plan, me, units, ranks, down, block=256):
    count, rows, width = units[0].shape
    total = 4 * rows
    rank = ranks[0].shape[1]
    return pl.pallas_call(
        functools.partial(attend_body, min(block, rows)),
        out_shape=[jax.ShapeDtypeStruct((4, rows, width), BF16)] * 4,
        in_specs=[SMEM, SMEM] + [ANY] * 9,
        out_specs=[ANY] * 4,
        scratch_shapes=[
            pltpu.VMEM((4, total, width), BF16),
            pltpu.VMEM((4, total, width), BF16),
            pltpu.VMEM((total, rank), BF16),
            pltpu.VMEM((width, rank), BF16),
            pltpu.VMEM((total, width), F32),
            pltpu.VMEM((total, width), F32),
            pltpu.SemaphoreType.DMA((4,)),
            pltpu.SemaphoreType.DMA((5,)),
            pltpu.SemaphoreType.DMA((4,)),
        ],
        compiler_params=pltpu.CompilerParams(vmem_limit_bytes=56 * 2**20),
        name="attend",
    )(plan, me, *units, *ranks, down)


def move(x, axis, target):
    count = lax.axis_size(axis)
    return lax.ppermute(x, axis, [(i, target(i) % count) for i in range(count)])


def up(x):
    return move(x, "ctx", lambda i: i + 1)


def down_one(x):
    return move(x, "ctx", lambda i: i - 1)


def cross(x):
    return move(x, "ctx", lambda i: i + 2 if i % 2 == 0 else i - 2)


def cross_back(x):
    return move(x, "ctx", lambda i: i - 2 if i % 2 == 0 else i + 2)


def sibling(x):
    return move(x, "head", lambda i: i ^ 1)


def far_exchange(case, pack, shape, dtype):
    def none():
        return jnp.zeros(shape, dtype)

    def one():
        x = pack()
        return x.at[0].set(lax.ppermute(x[0], "head", [(1, 3), (3, 1)]))

    def two():
        x = pack()
        return x.at[0].set(move(x[0], "head", lambda i: i ^ 2))

    def more():
        return move(pack(), "head", lambda i: i ^ 2)

    return lax.switch(case, (none, one, two, more))


def head_sum(x):
    x = x + sibling(x)
    return x + move(x, "head", lambda i: i ^ 2)


def head_gather(x, column):
    other = sibling(x)
    first = column % 2 == 0
    pair = jnp.concatenate([jnp.where(first, x, other), jnp.where(first, other, x)])
    far = move(pair, "head", lambda i: i ^ 2)
    low = column < 2
    return jnp.concatenate([jnp.where(low, pair, far), jnp.where(low, far, pair)])


def ctx_sum(x):
    count = lax.axis_size("ctx")
    parts = x.reshape(count, -1, 128)
    part = jnp.sum(lax.all_to_all(parts, "ctx", 0, 0, tiled=True), axis=0)
    every = jnp.broadcast_to(part[None], parts.shape)
    return lax.all_to_all(every, "ctx", 0, 0, tiled=True).reshape(x.shape)


def shards(
    inputs,
    queries,
    key_rows,
    value_rows,
    output_gradient,
    head_gradients,
    head_shift,
    down_qkv,
    up_qkv,
    output_down_adapter,
    up_out,
):
    rows_here, width = queries.shape
    heads_here = head_shift.shape[0]
    head_dim = width // heads_here
    place = lax.axis_index("ctx")
    column = lax.axis_index("head")
    me = jnp.stack([place, column]).astype(jnp.int32)
    own = (queries, key_rows, value_rows, head_gradients)
    with jax.named_scope("heads_in"):
        plan, case = make_plan(head_shift, me)
        case = case.reshape(())
        sib = tuple(sibling(x) for x in own)
        far_shape = (2, 4, rows_here, head_dim)
        far = far_exchange(case, lambda: far_pack(plan, own, head_dim), far_shape, BF16)
        slots = slot_pack(plan, own, sib, far, head_dim)
        units = (up(slots[1]), slots[0], down_one(slots[2]), cross(slots[3]))

    with jax.named_scope("ranks_in"):
        output_part = jnp.einsum(
            "td,rd->tr", output_gradient, up_out, preferred_element_type=F32
        )
        input_part = jnp.einsum("td,kdr->tkr", inputs, down_qkv, preferred_element_type=F32)
        rank_sum = head_sum(
            jnp.concatenate([input_part.reshape(rows_here, -1), output_part], axis=1)
        ).astype(BF16)
        rank = up_out.shape[0]
        input_lowrank = rank_sum[:, : 3 * rank].reshape(rows_here, 3, rank)
        output_rank = rank_sum[:, 3 * rank :]
        ranks = (up(output_rank), output_rank, down_one(output_rank), cross(output_rank))
        down_all = head_gather(output_down_adapter, column)

    results = attend(plan, me, units, ranks, down_all)

    with jax.named_scope("heads_back"):
        back = (
            results[1],
            down_one(results[0]),
            up(results[2]),
            cross_back(results[3]),
        )
        back_sib = tuple(sibling(x) for x in back)
        back_far = far_exchange(case, lambda: far_return_pack(plan, back), far_shape, BF16)
        projection_gradients, attention_result = head_unpack(
            plan, back, back_sib, back_far, heads_here
        )

    with jax.named_scope("adapters"):
        grad_part = jnp.einsum(
            "ktc,krc->tkr", projection_gradients, up_qkv, preferred_element_type=F32
        )
        out_part = jnp.einsum(
            "tc,cr->tr", attention_result, output_down_adapter, preferred_element_type=F32
        )
        back_sum = head_sum(
            jnp.concatenate([grad_part.reshape(rows_here, -1), out_part], axis=1)
        ).astype(BF16)
        projection_down = jnp.einsum(
            "nb,nj->bj", back_sum[:, : 3 * rank], inputs, preferred_element_type=F32
        )
        output_up = jnp.einsum(
            "nb,nj->bj", back_sum[:, 3 * rank :], output_gradient, preferred_element_type=F32
        )
        projection_up = jnp.einsum(
            "idy,dio->dyo", input_lowrank, projection_gradients, preferred_element_type=F32
        )
        output_down = jnp.einsum(
            "pq,pu->qu", output_rank, attention_result, preferred_element_type=F32
        )
        scale = adapter_scale * (rows_here * lax.axis_size("ctx")) ** (-0.5)
        wide = jnp.concatenate([projection_down, output_up], axis=0)
        narrow = jnp.concatenate([projection_up.reshape(3 * rank, width), output_down], axis=0)
        summed = scale * ctx_sum(jnp.concatenate([wide, narrow], axis=1))
        features = inputs.shape[1]
        wide, narrow = summed[:, :features], summed[:, features:]
    return (
        projection_gradients,
        wide[: 3 * rank].reshape(3, rank, features).transpose(0, 2, 1),
        narrow[: 3 * rank].reshape(3, rank, width),
        narrow[3 * rank :].T,
        wide[3 * rank :],
    )


def solution(mesh):
    placed = (
        P("ctx", "head"),
        P("ctx", "head"),
        P("ctx", "head"),
        P("ctx", "head"),
        P("ctx", "head"),
        P("ctx", "head"),
        P("head"),
        P(None, "head", None),
        P(None, None, "head"),
        P("head", None),
        P(None, "head"),
    )
    return jax.shard_map(
        shards,
        mesh=mesh,
        in_specs=placed,
        out_specs=(
            P(None, "ctx", "head"),
            P(None, "head", None),
            P(None, None, "head"),
            P("head", None),
            P(None, "head"),
        ),
        check_vma=False,
    )
```

```python
import functools

import jax
import jax.numpy as jnp
from jax import lax
from jax.experimental import pallas as pl
from jax.experimental.pallas import tpu as pltpu
from jax.sharding import PartitionSpec as P

adapter_scale = 2.0
F32 = jnp.float32
BF16 = jnp.bfloat16
ANY = pl.BlockSpec(memory_space=pl.ANY)
SMEM = pl.BlockSpec(memory_space=pltpu.SMEM)
VMEM = pl.BlockSpec(memory_space=pltpu.VMEM)
PARAMS = pltpu.CompilerParams(vmem_limit_bytes=40 * 2**20)

ROLE_OF_SLOT = ((3, 0, 2, 1), (0, 1, 3, 2), (1, 2, 0, 3), (2, 3, 1, 0))
SLOT_OF_ROLE = tuple(tuple(row.index(r) for r in range(4)) for row in ROLE_OF_SLOT)


def pick(index, values):
    out = jnp.int32(values[-1]) if isinstance(values[-1], int) else values[-1]
    for i in range(len(values) - 2, -1, -1):
        out = jnp.where(index == i, values[i], out)
    return out


def plan_kernel(own_ref, sib_ref, me_ref, out_ref, case_ref):
    place, column = me_ref[0], me_ref[1]
    quarter = lax.rem(place, 4)
    high, core = lax.div(column, 2), lax.rem(column, 2)

    def chip(near, other):
        first = [jnp.where(core == 0, near[i], other[i]) for i in range(4)]
        second = [jnp.where(core == 0, other[i], near[i]) for i in range(4)]
        return first + second

    mine = chip(own_ref, sib_ref)
    excess = sum(mine) - 4
    swaps = jnp.abs(excess)
    low_swaps = lax.div(swaps, 2)
    core_swaps = (low_swaps, swaps - low_swaps)
    sent_type = jnp.where(excess > 0, 1, jnp.where(excess < 0, 0, 1 - high))
    other_type = 1 - sent_type
    rank_sent = jnp.int32(0)
    rank_other = jnp.int32(0)
    kept, worker, role, column_rank = [], [], [], []
    for h in range(8):
        if h % 4 == 0:
            in_column = jnp.int32(0)
        is_sent = mine[h] == sent_type
        keep = jnp.logical_not(is_sent & (in_column < core_swaps[h // 4]))
        column_rank.append(in_column)
        at = jnp.where(is_sent, rank_sent, rank_other)
        room = 2 - core_swaps[0]
        on_core = jnp.where(is_sent, lax.div(at, 2), jnp.where(at < room, 0, 1))
        turn = jnp.where(is_sent, lax.rem(at, 2), jnp.where(at < room, at, at - room))
        kept.append(keep)
        worker.append(on_core)
        role.append(mine[h] * 2 + turn)
        in_column = in_column + jnp.where(is_sent, 1, 0)
        rank_sent = rank_sent + jnp.where(is_sent & keep, 1, 0)
        rank_other = rank_other + jnp.where(is_sent, 0, 1)
    source = [jnp.int32(9), jnp.int32(8), jnp.int32(9), jnp.int32(8)]
    for h in range(8):
        here = jnp.where(core == h // 4, h % 4, 4 + h % 4)
        for r in range(4):
            hit = kept[h] & (worker[h] == core) & (role[h] == r)
            source[r] = jnp.where(hit, here, source[r])
    slots = [pick(quarter, [ROLE_OF_SLOT[j][s] for j in range(4)]) for s in range(4)]
    for s in range(4):
        out_ref[s] = pick(slots[s], source)
    slot_of = [pick(quarter, [SLOT_OF_ROLE[j][r] for j in range(4)]) for r in range(4)]
    for want in range(2):
        out_index = jnp.int32(0)
        for i in range(4):
            own = jnp.where(core == 0, mine[i], mine[4 + i])
            rank = jnp.where(core == 0, column_rank[i], column_rank[4 + i])
            out_index = jnp.where((own == sent_type) & (rank == want), i, out_index)
        out_ref[4 + want] = out_index
    out_ref[6] = pick(other_type * 2 + 1, slot_of)
    out_ref[7] = pick(other_type * 2, slot_of)
    for i in range(4):
        keep = jnp.where(core == 0, kept[i], kept[4 + i])
        on_core = jnp.where(core == 0, worker[i], worker[4 + i])
        rank = jnp.where(core == 0, column_rank[i], column_rank[4 + i])
        which = jnp.where(core == 0, role[i], role[4 + i])
        back = pick(which, slot_of) + jnp.where(on_core == core, 0, 4)
        out_ref[8 + i] = jnp.where(keep, back, 8 + rank)
        near = lax.rem(which + 1, 4) + jnp.where(on_core == core, 0, 4)
        far = 8 + lax.rem(sent_type * 2 + 2 - rank, 4)
        out_ref[12 + i] = jnp.where(keep, near, far)
    case_ref[0] = jnp.where(swaps > 1, 1, 0)


def make_plan(shift, me):
    return pl.pallas_call(
        plan_kernel,
        out_shape=[jax.ShapeDtypeStruct((16,), jnp.int32), jax.ShapeDtypeStruct((1,), jnp.int32)],
        in_specs=[SMEM] * 3,
        out_specs=[SMEM] * 2,
        name="plan",
    )(shift, sibling(shift), me)


def column_of(ref, index, width):
    return ref.at[:, pl.ds(pl.multiple_of(index * width, width), width)]


def far_pack(plan, arrays, width, wanted):
    count = len(arrays)
    tops = [0]
    for array in arrays:
        tops.append(tops[-1] + array.shape[0])

    def body(plan_ref, *refs):
        own, outs, sems = refs[:count], refs[count:-1], refs[-1]
        copies = []
        for r in range(wanted):
            for t in range(count):
                copy = pltpu.make_async_copy(
                    column_of(own[t], plan_ref[4 + r], width),
                    outs[r].at[tops[t] : tops[t + 1]],
                    sems.at[r, t],
                )
                copy.start()
                copies.append(copy)
        for copy in copies:
            copy.wait()

    return pl.pallas_call(
        body,
        out_shape=[jax.ShapeDtypeStruct((tops[-1], width), BF16)] * wanted,
        in_specs=[SMEM] + [ANY] * count,
        out_specs=[VMEM] * wanted,
        scratch_shapes=[pltpu.SemaphoreType.DMA((wanted, count))],
        compiler_params=PARAMS,
        name="far_pack",
    )(plan, *arrays)


def slot_pack(plan, own_arrays, sibling_arrays, far, ranks, width):
    count = len(own_arrays) - 1
    rows = own_arrays[0].shape[0]
    adapter_rows = own_arrays[count].shape[0]
    rank_rows = ranks.shape[0]
    parts = rows // width

    def body(plan_ref, *refs):
        own, sib = refs[: count + 1], refs[count + 1 : 2 * count + 2]
        far_refs = refs[2 * count + 2 : 2 * count + 4]
        rank_ref = refs[2 * count + 4]
        outs = refs[2 * count + 5 : 2 * count + 9]
        adapter_ref, sems = refs[2 * count + 9], refs[2 * count + 10]

        def copy(s, t, source):
            if t < count:
                return pltpu.make_async_copy(
                    source, outs[s].at[t * rows : (t + 1) * rows], sems.at[s, t]
                )
            return pltpu.make_async_copy(source, adapter_ref, sems.at[s, t])

        def far_part(r, t):
            size = rows if t < count else adapter_rows
            return far_refs[r].at[t * rows : t * rows + size]

        for s in range(4):
            source = plan_ref[s]
            tensors = range(count + 1 if s == 0 else count)

            @pl.when(source < 4)
            def _(s=s, source=source, tensors=tensors):
                for t in tensors:
                    copy(s, t, column_of(own[t], source, width)).start()

            @pl.when((source >= 4) & (source < 8))
            def _(s=s, source=source, tensors=tensors):
                for t in tensors:
                    copy(s, t, column_of(sib[t], source - 4, width)).start()

            for r in range(2):

                @pl.when(source == 8 + r)
                def _(s=s, r=r, tensors=tensors):
                    for t in tensors:
                        copy(s, t, far_part(r, t)).start()

        for s in range(4):
            for i in range(parts):
                top = count * rows + i * rank_rows
                outs[s][top : top + rank_rows, :] = rank_ref[:, i * width : (i + 1) * width]
        for s in range(4):
            for t in range(count + 1 if s == 0 else count):
                copy(s, t, far_part(0, t)).wait()

    return pl.pallas_call(
        body,
        out_shape=[jax.ShapeDtypeStruct((count * rows + parts * rank_rows, width), BF16)] * 4
        + [jax.ShapeDtypeStruct((adapter_rows, width), BF16)],
        in_specs=[SMEM] + [ANY] * (2 * count + 4) + [VMEM],
        out_specs=[VMEM] * 5,
        scratch_shapes=[pltpu.SemaphoreType.DMA((4, count + 1))],
        compiler_params=PARAMS,
        name="slot_pack",
    )(plan, *own_arrays, *sibling_arrays, *far, ranks)


def far_return_pack(plan, slots, wanted):
    def body(plan_ref, *refs):
        ins, outs, sems = refs[:4], refs[4:-1], refs[-1]
        for r in range(wanted):
            for s in range(4):

                @pl.when(plan_ref[6 + r] == s)
                def _(r=r, s=s):
                    pltpu.make_async_copy(ins[s], outs[r], sems.at[r]).start()

        for r in range(wanted):
            pltpu.make_async_copy(ins[0], outs[r], sems.at[r]).wait()

    return pl.pallas_call(
        body,
        out_shape=[jax.ShapeDtypeStruct(slots[0].shape, BF16)] * wanted,
        in_specs=[SMEM] + [ANY] * 4,
        out_specs=[VMEM] * wanted,
        scratch_shapes=[pltpu.SemaphoreType.DMA((wanted,))],
        compiler_params=PARAMS,
        name="far_return_pack",
    )(plan, *slots)


def head_unpack(plan, own_slots, sibling_slots, far, heads, rows):
    width = own_slots[0].shape[1]

    def body(plan_ref, *refs):
        places, grads, sems = refs[:10], refs[10], refs[11]

        def copy(place, t, i):
            return pltpu.make_async_copy(
                place.at[t * rows : (t + 1) * rows],
                grads.at[t, :, i * width : (i + 1) * width],
                sems.at[i, t],
            )

        for i in range(heads):
            source = plan_ref[8 + i]
            for s in range(10):

                @pl.when(source == s)
                def _(i=i, s=s):
                    for t in range(3):
                        copy(places[s], t, i).start()

        for i in range(heads):
            for t in range(3):
                copy(places[0], t, i).wait()

    return pl.pallas_call(
        body,
        out_shape=jax.ShapeDtypeStruct((3, rows, heads * width), BF16),
        in_specs=[SMEM] + [ANY] * 10,
        out_specs=VMEM,
        scratch_shapes=[pltpu.SemaphoreType.DMA((heads, 3))],
        compiler_params=PARAMS,
        name="head_unpack",
    )(plan, *own_slots, *sibling_slots, *far)


def rank_add(slots, rows, rank):
    width = slots[0].shape[1]

    def body(a, b, c, d, out):
        for i in range(rows // width):
            here = slice(i * 4 * rank, (i + 1) * 4 * rank)
            out[:, i * width : (i + 1) * width] = sum(
                ref[here, :].astype(F32) for ref in (a, b, c, d)
            )

    return pl.pallas_call(
        body,
        out_shape=jax.ShapeDtypeStruct((4 * rank, rows), F32),
        in_specs=[VMEM] * 4,
        out_specs=VMEM,
        compiler_params=PARAMS,
        name="rank_add",
    )(*slots)


def fold(plan, me, near, far, inputs, output_gradient, made, rank):
    features = inputs.shape[1]
    width = made[0].shape[1]
    wide, heads = features // width, 4

    def body(plan_ref, me_ref, near_ref, far_ref, in_ref, grad_ref, m0, m1, m2, out):
        ranks = (near_ref[...] + far_ref[...]).astype(BF16)
        top = dot_nn(ranks[: 3 * rank], in_ref[...])
        low = dot_nn(ranks[3 * rank :], grad_ref[...])
        both = jnp.concatenate([top, low])
        for j in range(wide):
            out[:, j, :] = both[:, j * width : (j + 1) * width]
        quarter = lax.rem(me_ref[0], 4)
        for i in range(heads):
            code = plan_ref[12 + i]
            here = lax.rem(code, 4) == quarter
            origin = lax.div(code, 4)
            found = jnp.where(origin == 0, m0[...], jnp.where(origin == 1, m1[...], m2[...]))
            out[:, wide + i, :] = jnp.where(here, found, 0.0)

    return pl.pallas_call(
        body,
        out_shape=jax.ShapeDtypeStruct((4 * rank, wide + heads, width), F32),
        in_specs=[SMEM] * 2 + [VMEM] * 7,
        out_specs=VMEM,
        compiler_params=PARAMS,
        name="fold",
    )(plan, me, near, far, inputs, output_gradient, *made)


def sum_and_spread(parts, scale):
    def body(ref, out):
        total = scale * jnp.sum(ref[...], axis=0)
        out[...] = jnp.broadcast_to(total[None], out.shape)

    return pl.pallas_call(
        body,
        out_shape=jax.ShapeDtypeStruct(parts.shape, F32),
        in_specs=[VMEM],
        out_specs=VMEM,
        compiler_params=PARAMS,
        name="sum_and_spread",
    )(parts)


def unfold(every, rank, wide):
    rows, columns, width = every.shape
    heads = columns - wide

    def body(ref, down, up_grad, out_down, out_up):
        for j in range(columns):
            block = ref[:, j, :]
            at = j if j < wide else j - wide
            here = slice(at * width, (at + 1) * width)
            first, second = (down, out_up) if j < wide else (up_grad, out_down)
            for k in range(3):
                first[k, :, here] = block[k * rank : (k + 1) * rank]
            second[:, here] = block[3 * rank :]

    return pl.pallas_call(
        body,
        out_shape=[
            jax.ShapeDtypeStruct((3, rank, wide * width), F32),
            jax.ShapeDtypeStruct((3, rank, heads * width), F32),
            jax.ShapeDtypeStruct((rank, heads * width), F32),
            jax.ShapeDtypeStruct((rank, wide * width), F32),
        ],
        in_specs=[VMEM],
        out_specs=[VMEM] * 4,
        compiler_params=PARAMS,
        name="unfold",
    )(every)


def dot_nt(a, b):
    return lax.dot_general(a, b, (((1,), (1,)), ((), ())), preferred_element_type=F32)


def dot_nn(a, b):
    return lax.dot_general(a, b, (((1,), (0,)), ((), ())), preferred_element_type=F32)


def dot_tn(a, b):
    return lax.dot_general(a, b, (((0,), (0,)), ((), ())), preferred_element_type=F32)


def attend_body(
    block, rank, me_ref, adapter, left, own, right, far,
    out_l, out_o, out_r, out_f, rank_l, rank_o, rank_r, rank_f, narrow,
    held, ranks, made, key_sum, value_sum, rank_out, in_sems, rank_sems, out_sems,
):
    width = held.shape[2]
    total = held.shape[1]
    rows = total // 4
    parts = rows // width
    factor = width**-0.5
    odd = lax.rem(me_ref[0], 2)
    spots = [1 - odd, 2 - odd, 3 - odd, odd * 3]

    def at(i):
        return pl.ds(pl.multiple_of(spots[i] * rows, rows), rows)

    copies = []
    for i, source in enumerate((left, own, right, far)):
        for t in range(4):
            copy = pltpu.make_async_copy(
                source.at[t * rows : (t + 1) * rows], held.at[t, at(i)], in_sems.at[i, t]
            )
            copy.start()
            copies.append(copy)
        copy = pltpu.make_async_copy(
            source.at[4 * rows : 4 * rows + parts * 4 * rank], ranks.at[spots[i]], rank_sems.at[i]
        )
        copy.start()
        copies.append(copy)
    key_sum[...] = jnp.zeros_like(key_sum)
    value_sum[...] = jnp.zeros_like(value_sum)
    for copy in copies:
        copy.wait()
    down = adapter[3 * rank :, :]
    for p in range(4):
        for i in range(parts):
            here = pl.ds(p * rows + i * width, width)
            block_rank = ranks[p, i * 4 * rank + 3 * rank : (i + 1) * 4 * rank, :]
            held[3, here, :] = (
                held[3, here, :].astype(F32) + adapter_scale * dot_tn(block_rank, down)
            ).astype(BF16)
    mask = lax.broadcasted_iota(jnp.int32, (block, block), 1) <= lax.broadcasted_iota(
        jnp.int32, (block, block), 0
    )
    for i in reversed(range(total // block)):
        here = pl.ds(i * block, block)
        span = (i + 1) * block
        query, grad = held[0, here, :], held[3, here, :]
        keys, values = held[1, :span, :], held[2, :span, :]
        score = dot_nt(query, keys) * (factor * 1.4426950408889634)
        last = jnp.where(mask, score[:, i * block :], -1e30)
        score = jnp.concatenate([score[:, : i * block], last], axis=1) if i else last
        peak = jnp.max(score, axis=1, keepdims=True)
        weight = jnp.exp2(score - peak)
        attention = weight * (1.0 / jnp.sum(weight, axis=1, keepdims=True))
        attention_bf = attention.astype(BF16)
        out = dot_nn(attention_bf, values).astype(BF16)
        delta = jnp.sum(grad.astype(F32) * out.astype(F32), axis=1, keepdims=True)
        dscore = (attention * (dot_nt(grad, values) - delta)).astype(BF16)
        made[0, here, :] = (dot_nn(dscore, keys) * factor).astype(BF16)
        made[3, here, :] = out
        key_sum[:span, :] += dot_tn(dscore, query)
        value_sum[:span, :] += dot_tn(attention_bf, grad)
    made[1] = (key_sum[...] * factor).astype(BF16)
    made[2] = value_sum[...].astype(BF16)
    copies = []
    for i, target in enumerate((out_l, out_o, out_r, out_f)):
        for t in range(3):
            copy = pltpu.make_async_copy(
                made.at[t, at(i)], target.at[t * rows : (t + 1) * rows], out_sems.at[i, t]
            )
            copy.start()
            copies.append(copy)
    for t in range(4):
        mine = slice(t * rank, (t + 1) * rank)
        back = dot_nt(adapter[mine, :], made[t]).astype(BF16)
        rows_t = []
        for p in range(4):
            for i in range(parts):
                here = slice(i * 4 * rank + t * rank, i * 4 * rank + (t + 1) * rank)
                start = p * rows + i * width
                rank_out[p, here, :] = back[:, start : start + width]
                rows_t.append(ranks[p, here, :])
        narrow[mine, :] = dot_nn(jnp.concatenate(rows_t, axis=1), made[t])
    for i, target in enumerate((rank_l, rank_o, rank_r, rank_f)):
        copy = pltpu.make_async_copy(rank_out.at[spots[i]], target, rank_sems.at[i])
        copy.start()
        copies.append(copy)
    for copy in copies:
        copy.wait()


def attend(me, adapter, units, rows, rank, block=512):
    width = units[0].shape[1]
    total = 4 * rows
    parts = rows // width
    return pl.pallas_call(
        functools.partial(attend_body, min(block, rows), rank),
        out_shape=[jax.ShapeDtypeStruct((3 * rows, width), BF16)] * 4
        + [jax.ShapeDtypeStruct((parts * 4 * rank, width), BF16)] * 4
        + [jax.ShapeDtypeStruct((4 * rank, width), F32)],
        in_specs=[SMEM, VMEM] + [ANY] * 4,
        out_specs=[ANY] * 8 + [VMEM],
        scratch_shapes=[
            pltpu.VMEM((4, total, width), BF16),
            pltpu.VMEM((4, parts * 4 * rank, width), BF16),
            pltpu.VMEM((4, total, width), BF16),
            pltpu.VMEM((total, width), F32),
            pltpu.VMEM((total, width), F32),
            pltpu.VMEM((4, parts * 4 * rank, width), BF16),
            pltpu.SemaphoreType.DMA((4, 4)),
            pltpu.SemaphoreType.DMA((4,)),
            pltpu.SemaphoreType.DMA((4, 3)),
        ],
        compiler_params=pltpu.CompilerParams(vmem_limit_bytes=56 * 2**20),
        name="attend",
    )(me, adapter, *units)


def move(x, axis, target):
    count = lax.axis_size(axis)
    return lax.ppermute(x, axis, [(i, target(i) % count) for i in range(count)])


def up(x):
    return move(x, "ctx", lambda i: i + 1)


def down_one(x):
    return move(x, "ctx", lambda i: i - 1)


def cross(x):
    return move(x, "ctx", lambda i: i + 2 if i % 2 == 0 else i - 2)


def cross_back(x):
    return move(x, "ctx", lambda i: i - 2 if i % 2 == 0 else i + 2)


def sibling(x):
    return move(x, "head", lambda i: i ^ 1)


def far_first(x):
    return lax.ppermute(x, "head", [(1, 3), (3, 1)])


def far_others(first, traded):
    low = lax.ppermute(first[0], "head", [(0, 2), (2, 0)])
    second = move(first[1], "head", lambda i: i ^ 2)
    core = lax.rem(lax.axis_index("head"), 2)
    return jnp.where(core == 1, traded, low), second


def head_sum(x):
    x = x + sibling(x)
    return x + move(x, "head", lambda i: i ^ 2)


def ctx_trade(x):
    return lax.all_to_all(x, "ctx", 0, 0, tiled=True)


def shards(
    inputs,
    queries,
    key_rows,
    value_rows,
    output_gradient,
    head_gradients,
    head_shift,
    down_qkv,
    up_qkv,
    output_down_adapter,
    up_out,
):
    rows_here, width = queries.shape
    heads_here = head_shift.shape[0]
    head_dim = width // heads_here
    place = lax.axis_index("ctx")
    column = lax.axis_index("head")
    me = jnp.stack([place, column]).astype(jnp.int32)
    rank, features = up_out.shape
    adapter = jnp.concatenate([up_qkv.reshape(3 * rank, width), output_down_adapter.T])
    own = (queries, key_rows, value_rows, head_gradients, adapter)
    with jax.named_scope("heads_in"):
        plan, case = make_plan(head_shift, me)
        sib = tuple(sibling(x) for x in own)
        more = case.reshape(()) > 0
        leaving = far_pack(plan, own, head_dim, 1)[0]
        far = far_first(leaving)
        inputs_late, gradient_late, _ = lax.optimization_barrier(
            (inputs, output_gradient, leaving)
        )

    with jax.named_scope("ranks_in"):
        output_part = jnp.einsum(
            "td,rd->rt", gradient_late, up_out, preferred_element_type=F32
        )
        input_part = jnp.einsum("td,kdr->krt", inputs_late, down_qkv, preferred_element_type=F32)
        rank_part = jnp.concatenate([input_part.reshape(3 * rank, rows_here), output_part])
        ranks = head_sum(rank_part).astype(BF16)

    with jax.named_scope("units"):

        def plain():
            return slot_pack(plan, own, sib, (far, far), ranks, head_dim)

        def rest():
            traded = far_others(far_pack(plan, own, head_dim, 2), far)
            return slot_pack(plan, own, sib, traded, ranks, head_dim)

        slots = lax.cond(more, rest, plain)
        units = (up(slots[1]), slots[0], down_one(slots[2]), cross(slots[3]))
    results = attend(me, slots[4], units, rows_here, rank)

    with jax.named_scope("ranks_back"):
        pieces = (results[5], down_one(results[4]), up(results[6]), cross_back(results[7]))
        made = (results[8], sibling(results[8]), move(results[8], "head", lambda i: i ^ 2))
        pieces, made = lax.optimization_barrier((pieces, made))
        part = rank_add(pieces, rows_here, rank)
        part = part + sibling(part)
        other = move(part, "head", lambda i: i ^ 2)
        parts = fold(plan, me, part, other, inputs, output_gradient, made, rank)

    with jax.named_scope("heads_back"):
        back = (results[1], down_one(results[0]), up(results[2]), cross_back(results[3]))

    with jax.named_scope("heads_home"):
        back_sib = tuple(sibling(x) for x in back)
        back_far = far_first(far_return_pack(plan, back, 1)[0])

        def plain_back():
            far = (back_far, back_far)
            return head_unpack(plan, back, back_sib, far, heads_here, rows_here)

        def rest_back():
            traded = far_others(far_return_pack(plan, back, 2), back_far)
            return head_unpack(plan, back, back_sib, traded, heads_here, rows_here)

        projection_gradients = lax.cond(more, rest_back, plain_back)

    with jax.named_scope("token_sums"):
        scale = adapter_scale * (rows_here * lax.axis_size("ctx")) ** (-0.5)
        every = ctx_trade(sum_and_spread(ctx_trade(parts), scale))
        down, up_grad, out_down, out_up = unfold(every, rank, features // head_dim)

    return (projection_gradients, down.transpose(0, 2, 1), up_grad, out_down.T, out_up)


def solution(mesh):
    placed = (
        P("ctx", "head"),
        P("ctx", "head"),
        P("ctx", "head"),
        P("ctx", "head"),
        P("ctx", "head"),
        P("ctx", "head"),
        P("head"),
        P(None, "head", None),
        P(None, None, "head"),
        P("head", None),
        P(None, "head"),
    )
    return jax.shard_map(
        shards,
        mesh=mesh,
        in_specs=placed,
        out_specs=(
            P(None, "ctx", "head"),
            P(None, "head", None),
            P(None, None, "head"),
            P("head", None),
            P(None, "head"),
        ),
        check_vma=False,
    )
```

```python
import functools

import jax
import jax.numpy as jnp
from jax import lax
from jax.experimental import pallas as pl
from jax.experimental.pallas import tpu as pltpu
from jax.sharding import PartitionSpec as P

adapter_scale = 2.0
F32 = jnp.float32
BF16 = jnp.bfloat16
ANY = pl.BlockSpec(memory_space=pl.ANY)
SMEM = pl.BlockSpec(memory_space=pltpu.SMEM)
VMEM = pl.BlockSpec(memory_space=pltpu.VMEM)
PARAMS = pltpu.CompilerParams(vmem_limit_bytes=40 * 2**20)

ROLE_OF_SLOT = ((3, 0, 2, 1), (0, 1, 3, 2), (1, 2, 0, 3), (2, 3, 1, 0))
SLOT_OF_ROLE = tuple(tuple(row.index(r) for r in range(4)) for row in ROLE_OF_SLOT)


def pick(index, values):
    out = jnp.int32(values[-1]) if isinstance(values[-1], int) else values[-1]
    for i in range(len(values) - 2, -1, -1):
        out = jnp.where(index == i, values[i], out)
    return out


def plan_kernel(own_ref, sib_ref, me_ref, out_ref, case_ref):
    place, column = me_ref[0], me_ref[1]
    quarter = lax.rem(place, 4)
    high, core = lax.div(column, 2), lax.rem(column, 2)

    def chip(near, other):
        first = [jnp.where(core == 0, near[i], other[i]) for i in range(4)]
        second = [jnp.where(core == 0, other[i], near[i]) for i in range(4)]
        return first + second

    mine = chip(own_ref, sib_ref)
    excess = sum(mine) - 4
    swaps = jnp.abs(excess)
    low_swaps = lax.div(swaps, 2)
    core_swaps = (low_swaps, swaps - low_swaps)
    sent_type = jnp.where(excess > 0, 1, jnp.where(excess < 0, 0, 1 - high))
    other_type = 1 - sent_type
    rank_sent = jnp.int32(0)
    rank_other = jnp.int32(0)
    kept, worker, role, column_rank = [], [], [], []
    for h in range(8):
        if h % 4 == 0:
            in_column = jnp.int32(0)
        is_sent = mine[h] == sent_type
        keep = jnp.logical_not(is_sent & (in_column < core_swaps[h // 4]))
        column_rank.append(in_column)
        at = jnp.where(is_sent, rank_sent, rank_other)
        room = 2 - core_swaps[0]
        on_core = jnp.where(is_sent, lax.div(at, 2), jnp.where(at < room, 0, 1))
        turn = jnp.where(is_sent, lax.rem(at, 2), jnp.where(at < room, at, at - room))
        kept.append(keep)
        worker.append(on_core)
        role.append(mine[h] * 2 + turn)
        in_column = in_column + jnp.where(is_sent, 1, 0)
        rank_sent = rank_sent + jnp.where(is_sent & keep, 1, 0)
        rank_other = rank_other + jnp.where(is_sent, 0, 1)
    source = [jnp.int32(9), jnp.int32(8), jnp.int32(9), jnp.int32(8)]
    for h in range(8):
        here = jnp.where(core == h // 4, h % 4, 4 + h % 4)
        for r in range(4):
            hit = kept[h] & (worker[h] == core) & (role[h] == r)
            source[r] = jnp.where(hit, here, source[r])
    slots = [pick(quarter, [ROLE_OF_SLOT[j][s] for j in range(4)]) for s in range(4)]
    for s in range(4):
        out_ref[s] = pick(slots[s], source)
    slot_of = [pick(quarter, [SLOT_OF_ROLE[j][r] for j in range(4)]) for r in range(4)]
    for want in range(2):
        out_index = jnp.int32(0)
        for i in range(4):
            own = jnp.where(core == 0, mine[i], mine[4 + i])
            rank = jnp.where(core == 0, column_rank[i], column_rank[4 + i])
            out_index = jnp.where((own == sent_type) & (rank == want), i, out_index)
        out_ref[4 + want] = out_index
    out_ref[6] = pick(other_type * 2 + 1, slot_of)
    out_ref[7] = pick(other_type * 2, slot_of)
    for i in range(4):
        keep = jnp.where(core == 0, kept[i], kept[4 + i])
        on_core = jnp.where(core == 0, worker[i], worker[4 + i])
        rank = jnp.where(core == 0, column_rank[i], column_rank[4 + i])
        which = jnp.where(core == 0, role[i], role[4 + i])
        back = pick(which, slot_of) + jnp.where(on_core == core, 0, 4)
        out_ref[8 + i] = jnp.where(keep, back, 8 + rank)
        near = lax.rem(which + 1, 4) + jnp.where(on_core == core, 0, 4)
        far = 8 + lax.rem(sent_type * 2 + 2 - rank, 4)
        out_ref[12 + i] = jnp.where(keep, near, far)
    case_ref[0] = jnp.where(swaps > 1, 1, 0)


def make_plan(shift, me):
    return pl.pallas_call(
        plan_kernel,
        out_shape=[jax.ShapeDtypeStruct((16,), jnp.int32), jax.ShapeDtypeStruct((1,), jnp.int32)],
        in_specs=[SMEM] * 3,
        out_specs=[SMEM] * 2,
        name="plan",
    )(shift, sibling(shift), me)


def column_of(ref, index, width):
    return ref.at[:, pl.ds(pl.multiple_of(index * width, width), width)]


def far_pack(plan, arrays, width, wanted):
    count = len(arrays)
    tops = [0]
    for array in arrays:
        tops.append(tops[-1] + array.shape[0])

    def body(plan_ref, *refs):
        own, outs, sems = refs[:count], refs[count:-1], refs[-1]
        copies = []
        for r in range(wanted):
            for t in range(count):
                copy = pltpu.make_async_copy(
                    column_of(own[t], plan_ref[4 + r], width),
                    outs[r].at[tops[t] : tops[t + 1]],
                    sems.at[r, t],
                )
                copy.start()
                copies.append(copy)
        for copy in copies:
            copy.wait()

    return pl.pallas_call(
        body,
        out_shape=[jax.ShapeDtypeStruct((tops[-1], width), BF16)] * wanted,
        in_specs=[SMEM] + [ANY] * count,
        out_specs=[VMEM] * wanted,
        scratch_shapes=[pltpu.SemaphoreType.DMA((wanted, count))],
        compiler_params=PARAMS,
        name="far_pack",
    )(plan, *arrays)


def slot_pack(plan, own_arrays, sibling_arrays, far, ranks, width):
    count = len(own_arrays) - 1
    rows = own_arrays[0].shape[0]
    adapter_rows = own_arrays[count].shape[0]
    rank_rows = ranks.shape[0]
    parts = rows // width

    def body(plan_ref, *refs):
        own, sib = refs[: count + 1], refs[count + 1 : 2 * count + 2]
        far_refs = refs[2 * count + 2 : 2 * count + 4]
        rank_ref = refs[2 * count + 4]
        outs = refs[2 * count + 5 : 2 * count + 9]
        adapter_ref, sems = refs[2 * count + 9], refs[2 * count + 10]

        def copy(s, t, source):
            if t < count:
                return pltpu.make_async_copy(
                    source, outs[s].at[t * rows : (t + 1) * rows], sems.at[s, t]
                )
            return pltpu.make_async_copy(source, adapter_ref, sems.at[s, t])

        def far_part(r, t):
            size = rows if t < count else adapter_rows
            return far_refs[r].at[t * rows : t * rows + size]

        for s in range(4):
            source = plan_ref[s]
            tensors = range(count + 1 if s == 0 else count)

            @pl.when(source < 4)
            def _(s=s, source=source, tensors=tensors):
                for t in tensors:
                    copy(s, t, column_of(own[t], source, width)).start()

            @pl.when((source >= 4) & (source < 8))
            def _(s=s, source=source, tensors=tensors):
                for t in tensors:
                    copy(s, t, column_of(sib[t], source - 4, width)).start()

            for r in range(2):

                @pl.when(source == 8 + r)
                def _(s=s, r=r, tensors=tensors):
                    for t in tensors:
                        copy(s, t, far_part(r, t)).start()

        for s in range(4):
            for i in range(parts):
                top = count * rows + i * rank_rows
                outs[s][top : top + rank_rows, :] = rank_ref[:, i * width : (i + 1) * width]
        for s in range(4):
            for t in range(count + 1 if s == 0 else count):
                copy(s, t, far_part(0, t)).wait()

    return pl.pallas_call(
        body,
        out_shape=[jax.ShapeDtypeStruct((count * rows + parts * rank_rows, width), BF16)] * 4
        + [jax.ShapeDtypeStruct((adapter_rows, width), BF16)],
        in_specs=[SMEM] + [ANY] * (2 * count + 4) + [VMEM],
        out_specs=[VMEM] * 5,
        scratch_shapes=[pltpu.SemaphoreType.DMA((4, count + 1))],
        compiler_params=PARAMS,
        name="slot_pack",
    )(plan, *own_arrays, *sibling_arrays, *far, ranks)


HOME_ORDER = (3, 1, 2, 0)


def far_return_pack(plan, slots, wanted):
    def body(plan_ref, *refs):
        ins = [refs[HOME_ORDER.index(s)] for s in range(4)]
        outs, sems = refs[4:-1], refs[-1]
        for r in range(wanted):
            for s in range(4):

                @pl.when(plan_ref[6 + r] == s)
                def _(r=r, s=s):
                    pltpu.make_async_copy(ins[s], outs[r], sems.at[r]).start()

        for r in range(wanted):
            pltpu.make_async_copy(ins[0], outs[r], sems.at[r]).wait()

    return pl.pallas_call(
        body,
        out_shape=[jax.ShapeDtypeStruct(slots[0].shape, BF16)] * wanted,
        in_specs=[SMEM] + [ANY] * 4,
        out_specs=[VMEM] * wanted,
        scratch_shapes=[pltpu.SemaphoreType.DMA((wanted,))],
        compiler_params=PARAMS,
        name="far_return_pack",
    )(plan, *(slots[s] for s in HOME_ORDER))


def head_unpack(plan, own_slots, sibling_slots, far, heads, rows):
    width = own_slots[0].shape[1]

    def body(plan_ref, *refs):
        places, grads, sems = refs[:10], refs[10], refs[11]

        def copy(place, t, i):
            return pltpu.make_async_copy(
                place.at[t * rows : (t + 1) * rows],
                grads.at[t, :, i * width : (i + 1) * width],
                sems.at[i, t],
            )

        for i in range(heads):
            source = plan_ref[8 + i]
            for s in range(10):

                @pl.when(source == s)
                def _(i=i, s=s):
                    for t in range(3):
                        copy(places[s], t, i).start()

        for i in range(heads):
            for t in range(3):
                copy(places[0], t, i).wait()

    return pl.pallas_call(
        body,
        out_shape=jax.ShapeDtypeStruct((3, rows, heads * width), BF16),
        in_specs=[SMEM] + [ANY] * 10,
        out_specs=VMEM,
        scratch_shapes=[pltpu.SemaphoreType.DMA((heads, 3))],
        compiler_params=PARAMS,
        name="head_unpack",
    )(plan, *own_slots, *sibling_slots, *far)


def rank_add(slots, rows, rank):
    width = slots[0].shape[1]

    def body(a, b, c, d, out):
        for i in range(rows // width):
            here = slice(i * 4 * rank, (i + 1) * 4 * rank)
            out[:, i * width : (i + 1) * width] = sum(
                ref[here, :].astype(F32) for ref in (a, b, c, d)
            )

    return pl.pallas_call(
        body,
        out_shape=jax.ShapeDtypeStruct((4 * rank, rows), F32),
        in_specs=[VMEM] * 4,
        out_specs=VMEM,
        compiler_params=PARAMS,
        name="rank_add",
    )(*slots)


def fold(plan, me, near, far, inputs, output_gradient, made, rank):
    features = inputs.shape[1]
    width = made[0].shape[1]
    heads = 4

    def body(plan_ref, me_ref, near_ref, far_ref, in_ref, grad_ref, m0, m1, m2, out):
        ranks = (near_ref[...] + far_ref[...]).astype(BF16)
        out[: 3 * rank, :features] = dot_nn(ranks[: 3 * rank], in_ref[...])
        out[3 * rank :, :features] = dot_nn(ranks[3 * rank :], grad_ref[...])
        quarter = lax.rem(me_ref[0], 4)
        for i in range(heads):
            code = plan_ref[12 + i]
            here = lax.rem(code, 4) == quarter
            origin = lax.div(code, 4)
            found = jnp.where(origin == 0, m0[...], jnp.where(origin == 1, m1[...], m2[...]))
            start = features + i * width
            out[:, start : start + width] = jnp.where(here, found, 0.0)

    return pl.pallas_call(
        body,
        out_shape=jax.ShapeDtypeStruct((4 * rank, features + heads * width), F32),
        in_specs=[SMEM] * 2 + [VMEM] * 7,
        out_specs=VMEM,
        compiler_params=PARAMS,
        name="fold",
    )(plan, me, near, far, inputs, output_gradient, *made)


def sum_and_spread(parts, scale):
    def body(ref, out):
        total = scale * jnp.sum(ref[...], axis=0, keepdims=True)
        out[...] = jnp.broadcast_to(total, out.shape)

    return pl.pallas_call(
        body,
        out_shape=jax.ShapeDtypeStruct(parts.shape, F32),
        in_specs=[VMEM],
        out_specs=VMEM,
        compiler_params=PARAMS,
        name="sum_and_spread",
    )(parts)


def unfold(every, rank, features):
    rows, columns = every.shape
    narrow = columns - features

    def body(ref, down, up_grad, out_down, out_up):
        for k in range(3):
            here = slice(k * rank, (k + 1) * rank)
            down[k] = ref[here, :features]
            up_grad[k] = ref[here, features:]
        out_up[...] = ref[3 * rank :, :features]
        out_down[...] = ref[3 * rank :, features:]

    return pl.pallas_call(
        body,
        out_shape=[
            jax.ShapeDtypeStruct((3, rank, features), F32),
            jax.ShapeDtypeStruct((3, rank, narrow), F32),
            jax.ShapeDtypeStruct((rank, narrow), F32),
            jax.ShapeDtypeStruct((rank, features), F32),
        ],
        in_specs=[VMEM],
        out_specs=[VMEM] * 4,
        compiler_params=PARAMS,
        name="unfold",
    )(every)


def dot_nt(a, b):
    return lax.dot_general(a, b, (((1,), (1,)), ((), ())), preferred_element_type=F32)


def dot_nn(a, b):
    return lax.dot_general(a, b, (((1,), (0,)), ((), ())), preferred_element_type=F32)


def dot_tn(a, b):
    return lax.dot_general(a, b, (((0,), (0,)), ((), ())), preferred_element_type=F32)


def attend_body(
    block, rank, me_ref, adapter, far, left, right, own,
    out_l, out_o, out_r, out_f, rank_l, rank_o, rank_r, rank_f, narrow,
    held, ranks, made, key_sum, value_sum, rank_out, in_sems, rank_sems, out_sems,
):
    width = held.shape[2]
    total = held.shape[1]
    rows = total // 4
    parts = rows // width
    factor = width**-0.5
    odd = lax.rem(me_ref[0], 2)
    spots = [1 - odd, 2 - odd, 3 - odd, odd * 3]

    def at(i):
        return pl.ds(pl.multiple_of(spots[i] * rows, rows), rows)

    copies = []
    for i, source in enumerate((left, own, right, far)):
        for t in range(4):
            copy = pltpu.make_async_copy(
                source.at[t * rows : (t + 1) * rows], held.at[t, at(i)], in_sems.at[i, t]
            )
            copy.start()
            copies.append(copy)
        copy = pltpu.make_async_copy(
            source.at[4 * rows : 4 * rows + parts * 4 * rank], ranks.at[spots[i]], rank_sems.at[i]
        )
        copy.start()
        copies.append(copy)
    key_sum[...] = jnp.zeros_like(key_sum)
    value_sum[...] = jnp.zeros_like(value_sum)
    for copy in copies:
        copy.wait()
    down = adapter[3 * rank :, :]
    for p in range(4):
        for i in range(parts):
            here = pl.ds(p * rows + i * width, width)
            block_rank = ranks[p, i * 4 * rank + 3 * rank : (i + 1) * 4 * rank, :]
            held[3, here, :] = (
                held[3, here, :].astype(F32) + adapter_scale * dot_tn(block_rank, down)
            ).astype(BF16)
    mask = lax.broadcasted_iota(jnp.int32, (block, block), 1) <= lax.broadcasted_iota(
        jnp.int32, (block, block), 0
    )
    for i in reversed(range(total // block)):
        here = pl.ds(i * block, block)
        span = (i + 1) * block
        query, grad = held[0, here, :], held[3, here, :]
        keys, values = held[1, :span, :], held[2, :span, :]
        score = dot_nt(query, keys) * (factor * 1.4426950408889634)
        last = jnp.where(mask, score[:, i * block :], -1e30)
        score = jnp.concatenate([score[:, : i * block], last], axis=1) if i else last
        peak = jnp.max(score, axis=1, keepdims=True)
        weight = jnp.exp2(score - peak)
        attention = weight * (1.0 / jnp.sum(weight, axis=1, keepdims=True))
        attention_bf = attention.astype(BF16)
        out = dot_nn(attention_bf, values).astype(BF16)
        delta = jnp.sum(grad.astype(F32) * out.astype(F32), axis=1, keepdims=True)
        dscore = (attention * (dot_nt(grad, values) - delta)).astype(BF16)
        made[0, here, :] = (dot_nn(dscore, keys) * factor).astype(BF16)
        made[3, here, :] = out
        key_sum[:span, :] += dot_tn(dscore, query)
        value_sum[:span, :] += dot_tn(attention_bf, grad)
    made[1] = (key_sum[...] * factor).astype(BF16)
    made[2] = value_sum[...].astype(BF16)
    copies = []
    for i, target in enumerate((out_l, out_o, out_r, out_f)):
        for t in range(3):
            copy = pltpu.make_async_copy(
                made.at[t, at(i)], target.at[t * rows : (t + 1) * rows], out_sems.at[i, t]
            )
            copy.start()
            copies.append(copy)
    for t in range(4):
        mine = slice(t * rank, (t + 1) * rank)
        back = dot_nt(adapter[mine, :], made[t]).astype(BF16)
        rows_t = []
        for p in range(4):
            for i in range(parts):
                here = slice(i * 4 * rank + t * rank, i * 4 * rank + (t + 1) * rank)
                start = p * rows + i * width
                rank_out[p, here, :] = back[:, start : start + width]
                rows_t.append(ranks[p, here, :])
        narrow[mine, :] = dot_nn(jnp.concatenate(rows_t, axis=1), made[t])
    for i, target in enumerate((rank_l, rank_o, rank_r, rank_f)):
        copy = pltpu.make_async_copy(rank_out.at[spots[i]], target, rank_sems.at[i])
        copy.start()
        copies.append(copy)
    for copy in copies:
        copy.wait()


def attend(me, adapter, units, rows, rank, block=512):
    width = units[0].shape[1]
    total = 4 * rows
    parts = rows // width
    return pl.pallas_call(
        functools.partial(attend_body, min(block, rows), rank),
        out_shape=[jax.ShapeDtypeStruct((3 * rows, width), BF16)] * 4
        + [jax.ShapeDtypeStruct((parts * 4 * rank, width), BF16)] * 4
        + [jax.ShapeDtypeStruct((4 * rank, width), F32)],
        in_specs=[SMEM, VMEM] + [ANY] * 4,
        out_specs=[ANY] * 8 + [VMEM],
        scratch_shapes=[
            pltpu.VMEM((4, total, width), BF16),
            pltpu.VMEM((4, parts * 4 * rank, width), BF16),
            pltpu.VMEM((4, total, width), BF16),
            pltpu.VMEM((total, width), F32),
            pltpu.VMEM((total, width), F32),
            pltpu.VMEM((4, parts * 4 * rank, width), BF16),
            pltpu.SemaphoreType.DMA((4, 4)),
            pltpu.SemaphoreType.DMA((4,)),
            pltpu.SemaphoreType.DMA((4, 3)),
        ],
        compiler_params=pltpu.CompilerParams(vmem_limit_bytes=56 * 2**20),
        name="attend",
    )(me, adapter, *units)


def move(x, axis, target):
    count = lax.axis_size(axis)
    return lax.ppermute(x, axis, [(i, target(i) % count) for i in range(count)])


def up(x):
    return move(x, "ctx", lambda i: i + 1)


def down_one(x):
    return move(x, "ctx", lambda i: i - 1)


def cross(x):
    return move(x, "ctx", lambda i: i + 2 if i % 2 == 0 else i - 2)


def cross_back(x):
    return move(x, "ctx", lambda i: i - 2 if i % 2 == 0 else i + 2)


def sibling(x):
    return move(x, "head", lambda i: i ^ 1)


def far_first(x):
    return lax.ppermute(x, "head", [(1, 3), (3, 1)])


def far_others(first, traded):
    low = lax.ppermute(first[0], "head", [(0, 2), (2, 0)])
    second = move(first[1], "head", lambda i: i ^ 2)
    core = lax.rem(lax.axis_index("head"), 2)
    return jnp.where(core == 1, traded, low), second


def head_sum(x):
    x = x + sibling(x)
    return x + move(x, "head", lambda i: i ^ 2)


def ctx_trade(x):
    return lax.all_to_all(x, "ctx", 0, 0, tiled=True)


def shards(
    inputs,
    queries,
    key_rows,
    value_rows,
    output_gradient,
    head_gradients,
    head_shift,
    down_qkv,
    up_qkv,
    output_down_adapter,
    up_out,
):
    rows_here, width = queries.shape
    heads_here = head_shift.shape[0]
    head_dim = width // heads_here
    place = lax.axis_index("ctx")
    column = lax.axis_index("head")
    me = jnp.stack([place, column]).astype(jnp.int32)
    rank, features = up_out.shape
    adapter = jnp.concatenate([up_qkv.reshape(3 * rank, width), output_down_adapter.T])
    own = (queries, key_rows, value_rows, head_gradients, adapter)
    with jax.named_scope("heads_in"):
        plan, case = make_plan(head_shift, me)
        sib = tuple(sibling(x) for x in own)
        more = case.reshape(()) > 0
        leaving = far_pack(plan, own, head_dim, 1)[0]
        far = far_first(leaving)
        inputs_late, gradient_late, _ = lax.optimization_barrier(
            (inputs, output_gradient, leaving)
        )

    with jax.named_scope("ranks_in"):
        output_part = jnp.einsum(
            "td,rd->rt", gradient_late, up_out, preferred_element_type=F32
        )
        input_part = jnp.einsum("td,kdr->krt", inputs_late, down_qkv, preferred_element_type=F32)
        rank_part = jnp.concatenate([input_part.reshape(3 * rank, rows_here), output_part])
        ranks = head_sum(rank_part).astype(BF16)

    with jax.named_scope("units"):

        def plain(far, sib, own, ranks, plan):
            return slot_pack(plan, own, sib, (far, far), ranks, head_dim)

        def rest(far, sib, own, ranks, plan):
            traded = far_others(far_pack(plan, own, head_dim, 2), far)
            return slot_pack(plan, own, sib, traded, ranks, head_dim)

        slots = lax.cond(more, rest, plain, far, sib, own, ranks, plan)
        units = (cross(slots[3]), up(slots[1]), down_one(slots[2]), slots[0])
    results = attend(me, slots[4], units, rows_here, rank)

    with jax.named_scope("ranks_back"):
        pieces = (cross_back(results[7]), down_one(results[4]), up(results[6]), results[5])
        made = (results[8], sibling(results[8]), move(results[8], "head", lambda i: i ^ 2))
        pieces, made = lax.optimization_barrier((pieces, made))
        part = rank_add(pieces, rows_here, rank)
        part = part + sibling(part)
        other = move(part, "head", lambda i: i ^ 2)
        parts = fold(plan, me, part, other, inputs, output_gradient, made, rank)

    with jax.named_scope("heads_back"):
        crossed = cross_back(results[3])
        back = (results[1], down_one(results[0]), up(results[2]), crossed)

    with jax.named_scope("heads_home"):
        moved = {s: sibling(back[s]) for s in HOME_ORDER}
        back_sib = tuple(moved[s] for s in range(4))
        back_far = far_first(far_return_pack(plan, back, 1)[0])

        def plain_back():
            far = (back_far, back_far)
            return head_unpack(plan, back, back_sib, far, heads_here, rows_here)

        def rest_back():
            traded = far_others(far_return_pack(plan, back, 2), back_far)
            return head_unpack(plan, back, back_sib, traded, heads_here, rows_here)

        projection_gradients = lax.cond(more, rest_back, plain_back)

    with jax.named_scope("token_sums"):
        scale = adapter_scale * (rows_here * lax.axis_size("ctx")) ** (-0.5)
        every = ctx_trade(sum_and_spread(ctx_trade(parts), scale))
        down, up_grad, out_down, out_up = unfold(every, rank, features)

    return (projection_gradients, down.transpose(0, 2, 1), up_grad, out_down.T, out_up)


def solution(mesh):
    placed = (
        P("ctx", "head"),
        P("ctx", "head"),
        P("ctx", "head"),
        P("ctx", "head"),
        P("ctx", "head"),
        P("ctx", "head"),
        P("head"),
        P(None, "head", None),
        P(None, None, "head"),
        P("head", None),
        P(None, "head"),
    )
    return jax.shard_map(
        shards,
        mesh=mesh,
        in_specs=placed,
        out_specs=(
            P(None, "ctx", "head"),
            P(None, "head", None),
            P(None, None, "head"),
            P("head", None),
            P(None, "head"),
        ),
        check_vma=False,
    )
```

```python
import functools

import jax
import jax.numpy as jnp
from jax import lax
from jax.experimental import pallas as pl
from jax.experimental.pallas import tpu as pltpu
from jax.sharding import PartitionSpec as P

adapter_scale = 2.0
F32 = jnp.float32
BF16 = jnp.bfloat16
ANY = pl.BlockSpec(memory_space=pl.ANY)
SMEM = pl.BlockSpec(memory_space=pltpu.SMEM)
VMEM = pl.BlockSpec(memory_space=pltpu.VMEM)
PARAMS = pltpu.CompilerParams(vmem_limit_bytes=40 * 2**20)

ROLE_OF_SLOT = ((3, 0, 2, 1), (0, 1, 3, 2), (1, 2, 0, 3), (2, 3, 1, 0))
SLOT_OF_ROLE = tuple(tuple(row.index(r) for r in range(4)) for row in ROLE_OF_SLOT)


def pick(index, values):
    out = jnp.int32(values[-1]) if isinstance(values[-1], int) else values[-1]
    for i in range(len(values) - 2, -1, -1):
        out = jnp.where(index == i, values[i], out)
    return out


def plan_kernel(own_ref, sib_ref, me_ref, out_ref, case_ref):
    place, column = me_ref[0], me_ref[1]
    quarter = lax.rem(place, 4)
    high, core = lax.div(column, 2), lax.rem(column, 2)

    def chip(near, other):
        first = [jnp.where(core == 0, near[i], other[i]) for i in range(4)]
        second = [jnp.where(core == 0, other[i], near[i]) for i in range(4)]
        return first + second

    mine = chip(own_ref, sib_ref)
    excess = sum(mine) - 4
    swaps = jnp.abs(excess)
    low_swaps = lax.div(swaps, 2)
    core_swaps = (low_swaps, swaps - low_swaps)
    sent_type = jnp.where(excess > 0, 1, jnp.where(excess < 0, 0, 1 - high))
    other_type = 1 - sent_type
    rank_sent = jnp.int32(0)
    rank_other = jnp.int32(0)
    kept, worker, role, column_rank = [], [], [], []
    for h in range(8):
        if h % 4 == 0:
            in_column = jnp.int32(0)
        is_sent = mine[h] == sent_type
        keep = jnp.logical_not(is_sent & (in_column < core_swaps[h // 4]))
        column_rank.append(in_column)
        at = jnp.where(is_sent, rank_sent, rank_other)
        room = 2 - core_swaps[0]
        on_core = jnp.where(is_sent, lax.div(at, 2), jnp.where(at < room, 0, 1))
        turn = jnp.where(is_sent, lax.rem(at, 2), jnp.where(at < room, at, at - room))
        kept.append(keep)
        worker.append(on_core)
        role.append(mine[h] * 2 + turn)
        in_column = in_column + jnp.where(is_sent, 1, 0)
        rank_sent = rank_sent + jnp.where(is_sent & keep, 1, 0)
        rank_other = rank_other + jnp.where(is_sent, 0, 1)
    source = [jnp.int32(9), jnp.int32(8), jnp.int32(9), jnp.int32(8)]
    for h in range(8):
        here = jnp.where(core == h // 4, h % 4, 4 + h % 4)
        for r in range(4):
            hit = kept[h] & (worker[h] == core) & (role[h] == r)
            source[r] = jnp.where(hit, here, source[r])
    slots = [pick(quarter, [ROLE_OF_SLOT[j][s] for j in range(4)]) for s in range(4)]
    for s in range(4):
        out_ref[s] = pick(slots[s], source)
    slot_of = [pick(quarter, [SLOT_OF_ROLE[j][r] for j in range(4)]) for r in range(4)]
    for want in range(2):
        out_index = jnp.int32(0)
        for i in range(4):
            own = jnp.where(core == 0, mine[i], mine[4 + i])
            rank = jnp.where(core == 0, column_rank[i], column_rank[4 + i])
            out_index = jnp.where((own == sent_type) & (rank == want), i, out_index)
        out_ref[4 + want] = out_index
    out_ref[6] = pick(other_type * 2 + 1, slot_of)
    out_ref[7] = pick(other_type * 2, slot_of)
    for i in range(4):
        keep = jnp.where(core == 0, kept[i], kept[4 + i])
        on_core = jnp.where(core == 0, worker[i], worker[4 + i])
        rank = jnp.where(core == 0, column_rank[i], column_rank[4 + i])
        which = jnp.where(core == 0, role[i], role[4 + i])
        back = pick(which, slot_of) + jnp.where(on_core == core, 0, 4)
        out_ref[8 + i] = jnp.where(keep, back, 8 + rank)
        near = lax.rem(which + 1, 4) + jnp.where(on_core == core, 0, 4)
        far = 8 + lax.rem(sent_type * 2 + 2 - rank, 4)
        out_ref[12 + i] = jnp.where(keep, near, far)
    case_ref[0] = jnp.clip(swaps - 1, 0, 2)


def make_plan(shift, me):
    return pl.pallas_call(
        plan_kernel,
        out_shape=[jax.ShapeDtypeStruct((16,), jnp.int32), jax.ShapeDtypeStruct((1,), jnp.int32)],
        in_specs=[SMEM] * 3,
        out_specs=[SMEM] * 2,
        name="plan",
    )(shift, sibling(shift), me)


def column_of(ref, index, width):
    return ref.at[:, pl.ds(pl.multiple_of(index * width, width), width)]


def far_pack(plan, arrays, width, wanted):
    count = len(arrays)
    tops = [0]
    for array in arrays:
        tops.append(tops[-1] + array.shape[0])

    def body(plan_ref, *refs):
        own, outs, sems = refs[:count], refs[count:-1], refs[-1]
        copies = []
        for r in range(wanted):
            for t in range(count):
                copy = pltpu.make_async_copy(
                    column_of(own[t], plan_ref[4 + r], width),
                    outs[r].at[tops[t] : tops[t + 1]],
                    sems.at[r, t],
                )
                copy.start()
                copies.append(copy)
        for copy in copies:
            copy.wait()

    return pl.pallas_call(
        body,
        out_shape=[jax.ShapeDtypeStruct((tops[-1], width), BF16)] * wanted,
        in_specs=[SMEM] + [ANY] * count,
        out_specs=[VMEM] * wanted,
        scratch_shapes=[pltpu.SemaphoreType.DMA((wanted, count))],
        compiler_params=PARAMS,
        name="far_pack",
    )(plan, *arrays)


def slot_pack(plan, own_arrays, sibling_arrays, far, ranks, width):
    count = len(own_arrays) - 1
    rows = own_arrays[0].shape[0]
    adapter_rows = own_arrays[count].shape[0]
    rank_rows = ranks.shape[0]
    parts = rows // width

    def body(plan_ref, *refs):
        own, sib = refs[: count + 1], refs[count + 1 : 2 * count + 2]
        far_refs = refs[2 * count + 2 : 2 * count + 4]
        rank_ref = refs[2 * count + 4]
        outs = refs[2 * count + 5 : 2 * count + 9]
        adapter_ref, sems = refs[2 * count + 9], refs[2 * count + 10]

        def copy(s, t, source):
            if t < count:
                return pltpu.make_async_copy(
                    source, outs[s].at[t * rows : (t + 1) * rows], sems.at[s, t]
                )
            return pltpu.make_async_copy(source, adapter_ref, sems.at[s, t])

        def far_part(r, t):
            size = rows if t < count else adapter_rows
            return far_refs[r].at[t * rows : t * rows + size]

        for s in range(4):
            source = plan_ref[s]
            tensors = range(count + 1 if s == 0 else count)

            @pl.when(source < 4)
            def _(s=s, source=source, tensors=tensors):
                for t in tensors:
                    copy(s, t, column_of(own[t], source, width)).start()

            @pl.when((source >= 4) & (source < 8))
            def _(s=s, source=source, tensors=tensors):
                for t in tensors:
                    copy(s, t, column_of(sib[t], source - 4, width)).start()

            for r in range(2):

                @pl.when(source == 8 + r)
                def _(s=s, r=r, tensors=tensors):
                    for t in tensors:
                        copy(s, t, far_part(r, t)).start()

        for s in range(4):
            for i in range(parts):
                top = count * rows + i * rank_rows
                outs[s][top : top + rank_rows, :] = rank_ref[:, i * width : (i + 1) * width]
        for s in range(4):
            for t in range(count + 1 if s == 0 else count):
                copy(s, t, far_part(0, t)).wait()

    return pl.pallas_call(
        body,
        out_shape=[jax.ShapeDtypeStruct((count * rows + parts * rank_rows, width), BF16)] * 4
        + [jax.ShapeDtypeStruct((adapter_rows, width), BF16)],
        in_specs=[SMEM] + [ANY] * (2 * count + 4) + [VMEM],
        out_specs=[VMEM] * 5,
        scratch_shapes=[pltpu.SemaphoreType.DMA((4, count + 1))],
        compiler_params=PARAMS,
        name="slot_pack",
    )(plan, *own_arrays, *sibling_arrays, *far, ranks)


HOME_ORDER = (3, 1, 2, 0)


def far_return_pack(plan, slots, wanted):
    def body(plan_ref, *refs):
        ins = [refs[HOME_ORDER.index(s)] for s in range(4)]
        outs, sems = refs[4:-1], refs[-1]
        for r in range(wanted):
            for s in range(4):

                @pl.when(plan_ref[6 + r] == s)
                def _(r=r, s=s):
                    pltpu.make_async_copy(ins[s], outs[r], sems.at[r]).start()

        for r in range(wanted):
            pltpu.make_async_copy(ins[0], outs[r], sems.at[r]).wait()

    return pl.pallas_call(
        body,
        out_shape=[jax.ShapeDtypeStruct(slots[0].shape, BF16)] * wanted,
        in_specs=[SMEM] + [ANY] * 4,
        out_specs=[VMEM] * wanted,
        scratch_shapes=[pltpu.SemaphoreType.DMA((wanted,))],
        compiler_params=PARAMS,
        name="far_return_pack",
    )(plan, *(slots[s] for s in HOME_ORDER))


def head_unpack(plan, own_slots, sibling_slots, far, heads, rows):
    width = own_slots[0].shape[1]

    def body(plan_ref, *refs):
        places, grads, sems = refs[:10], refs[10], refs[11]

        def copy(place, t, i):
            return pltpu.make_async_copy(
                place.at[t * rows : (t + 1) * rows],
                grads.at[t, :, i * width : (i + 1) * width],
                sems.at[i, t],
            )

        for i in range(heads):
            source = plan_ref[8 + i]
            for s in range(10):

                @pl.when(source == s)
                def _(i=i, s=s):
                    for t in range(3):
                        copy(places[s], t, i).start()

        for i in range(heads):
            for t in range(3):
                copy(places[0], t, i).wait()

    return pl.pallas_call(
        body,
        out_shape=jax.ShapeDtypeStruct((3, rows, heads * width), BF16),
        in_specs=[SMEM] + [ANY] * 10,
        out_specs=VMEM,
        scratch_shapes=[pltpu.SemaphoreType.DMA((heads, 3))],
        compiler_params=PARAMS,
        name="head_unpack",
    )(plan, *own_slots, *sibling_slots, *far)


def rank_add(slots, rows, rank):
    width = slots[0].shape[1]

    def body(a, b, c, d, out):
        for i in range(rows // width):
            here = slice(i * 4 * rank, (i + 1) * 4 * rank)
            out[:, i * width : (i + 1) * width] = sum(
                ref[here, :].astype(F32) for ref in (a, b, c, d)
            )

    return pl.pallas_call(
        body,
        out_shape=jax.ShapeDtypeStruct((4 * rank, rows), F32),
        in_specs=[VMEM] * 4,
        out_specs=VMEM,
        compiler_params=PARAMS,
        name="rank_add",
    )(*slots)


def fold(plan, me, near, far, inputs, output_gradient, made, rank):
    features = inputs.shape[1]
    width = made[0].shape[1]
    heads = 4

    def body(plan_ref, me_ref, near_ref, far_ref, in_ref, grad_ref, m0, m1, m2, out):
        ranks = (near_ref[...] + far_ref[...]).astype(BF16)
        out[: 3 * rank, :features] = dot_nn(ranks[: 3 * rank], in_ref[...])
        out[3 * rank :, :features] = dot_nn(ranks[3 * rank :], grad_ref[...])
        quarter = lax.rem(me_ref[0], 4)
        for i in range(heads):
            code = plan_ref[12 + i]
            here = lax.rem(code, 4) == quarter
            origin = lax.div(code, 4)
            found = jnp.where(origin == 0, m0[...], jnp.where(origin == 1, m1[...], m2[...]))
            start = features + i * width
            out[:, start : start + width] = jnp.where(here, found, 0.0)

    return pl.pallas_call(
        body,
        out_shape=jax.ShapeDtypeStruct((4 * rank, features + heads * width), F32),
        in_specs=[SMEM] * 2 + [VMEM] * 7,
        out_specs=VMEM,
        compiler_params=PARAMS,
        name="fold",
    )(plan, me, near, far, inputs, output_gradient, *made)


def sum_and_spread(parts, scale):
    def body(ref, out):
        total = scale * jnp.sum(ref[...], axis=0, keepdims=True)
        out[...] = jnp.broadcast_to(total, out.shape)

    return pl.pallas_call(
        body,
        out_shape=jax.ShapeDtypeStruct(parts.shape, F32),
        in_specs=[VMEM],
        out_specs=VMEM,
        compiler_params=PARAMS,
        name="sum_and_spread",
    )(parts)


def unfold(every, rank, features):
    rows, columns = every.shape
    narrow = columns - features

    def body(ref, down, up_grad, out_down, out_up):
        for k in range(3):
            here = slice(k * rank, (k + 1) * rank)
            down[k] = ref[here, :features]
            up_grad[k] = ref[here, features:]
        out_up[...] = ref[3 * rank :, :features]
        out_down[...] = ref[3 * rank :, features:]

    return pl.pallas_call(
        body,
        out_shape=[
            jax.ShapeDtypeStruct((3, rank, features), F32),
            jax.ShapeDtypeStruct((3, rank, narrow), F32),
            jax.ShapeDtypeStruct((rank, narrow), F32),
            jax.ShapeDtypeStruct((rank, features), F32),
        ],
        in_specs=[VMEM],
        out_specs=[VMEM] * 4,
        compiler_params=PARAMS,
        name="unfold",
    )(every)


def dot_nt(a, b):
    return lax.dot_general(a, b, (((1,), (1,)), ((), ())), preferred_element_type=F32)


def dot_nn(a, b):
    return lax.dot_general(a, b, (((1,), (0,)), ((), ())), preferred_element_type=F32)


def dot_tn(a, b):
    return lax.dot_general(a, b, (((0,), (0,)), ((), ())), preferred_element_type=F32)


def attend_body(
    block, rank, me_ref, adapter, far, left, right, own,
    out_l, out_o, out_r, out_f, rank_l, rank_o, rank_r, rank_f, narrow,
    held, ranks, made, key_sum, value_sum, rank_out, in_sems, rank_sems, out_sems,
):
    width = held.shape[2]
    total = held.shape[1]
    rows = total // 4
    parts = rows // width
    factor = width**-0.5
    odd = lax.rem(me_ref[0], 2)
    spots = [1 - odd, 2 - odd, 3 - odd, odd * 3]

    def at(i):
        return pl.ds(pl.multiple_of(spots[i] * rows, rows), rows)

    copies = []
    for i, source in enumerate((left, own, right, far)):
        for t in range(4):
            copy = pltpu.make_async_copy(
                source.at[t * rows : (t + 1) * rows], held.at[t, at(i)], in_sems.at[i, t]
            )
            copy.start()
            copies.append(copy)
        copy = pltpu.make_async_copy(
            source.at[4 * rows : 4 * rows + parts * 4 * rank], ranks.at[spots[i]], rank_sems.at[i]
        )
        copy.start()
        copies.append(copy)
    key_sum[...] = jnp.zeros_like(key_sum)
    value_sum[...] = jnp.zeros_like(value_sum)
    for copy in copies:
        copy.wait()
    down = adapter[3 * rank :, :]
    for p in range(4):
        for i in range(parts):
            here = pl.ds(p * rows + i * width, width)
            block_rank = ranks[p, i * 4 * rank + 3 * rank : (i + 1) * 4 * rank, :]
            held[3, here, :] = (
                held[3, here, :].astype(F32) + adapter_scale * dot_tn(block_rank, down)
            ).astype(BF16)
    mask = lax.broadcasted_iota(jnp.int32, (block, block), 1) <= lax.broadcasted_iota(
        jnp.int32, (block, block), 0
    )
    for i in reversed(range(total // block)):
        here = pl.ds(i * block, block)
        span = (i + 1) * block
        query, grad = held[0, here, :], held[3, here, :]
        keys, values = held[1, :span, :], held[2, :span, :]
        score = dot_nt(query, keys) * (factor * 1.4426950408889634)
        last = jnp.where(mask, score[:, i * block :], -1e30)
        score = jnp.concatenate([score[:, : i * block], last], axis=1) if i else last
        peak = jnp.max(score, axis=1, keepdims=True)
        weight = jnp.exp2(score - peak)
        attention = weight * (1.0 / jnp.sum(weight, axis=1, keepdims=True))
        attention_bf = attention.astype(BF16)
        out = dot_nn(attention_bf, values).astype(BF16)
        delta = jnp.sum(grad.astype(F32) * out.astype(F32), axis=1, keepdims=True)
        dscore = (attention * (dot_nt(grad, values) - delta)).astype(BF16)
        made[0, here, :] = (dot_nn(dscore, keys) * factor).astype(BF16)
        made[3, here, :] = out
        key_sum[:span, :] += dot_tn(dscore, query)
        value_sum[:span, :] += dot_tn(attention_bf, grad)
    made[1] = (key_sum[...] * factor).astype(BF16)
    made[2] = value_sum[...].astype(BF16)
    copies = []
    for i, target in enumerate((out_l, out_o, out_r, out_f)):
        for t in range(3):
            copy = pltpu.make_async_copy(
                made.at[t, at(i)], target.at[t * rows : (t + 1) * rows], out_sems.at[i, t]
            )
            copy.start()
            copies.append(copy)
    for t in range(4):
        mine = slice(t * rank, (t + 1) * rank)
        back = dot_nt(adapter[mine, :], made[t]).astype(BF16)
        rows_t = []
        for p in range(4):
            for i in range(parts):
                here = slice(i * 4 * rank + t * rank, i * 4 * rank + (t + 1) * rank)
                start = p * rows + i * width
                rank_out[p, here, :] = back[:, start : start + width]
                rows_t.append(ranks[p, here, :])
        narrow[mine, :] = dot_nn(jnp.concatenate(rows_t, axis=1), made[t])
    for i, target in enumerate((rank_l, rank_o, rank_r, rank_f)):
        copy = pltpu.make_async_copy(rank_out.at[spots[i]], target, rank_sems.at[i])
        copy.start()
        copies.append(copy)
    for copy in copies:
        copy.wait()


def attend(me, adapter, units, rows, rank, block=512):
    width = units[0].shape[1]
    total = 4 * rows
    parts = rows // width
    return pl.pallas_call(
        functools.partial(attend_body, min(block, rows), rank),
        out_shape=[jax.ShapeDtypeStruct((3 * rows, width), BF16)] * 4
        + [jax.ShapeDtypeStruct((parts * 4 * rank, width), BF16)] * 4
        + [jax.ShapeDtypeStruct((4 * rank, width), F32)],
        in_specs=[SMEM, VMEM] + [ANY] * 4,
        out_specs=[ANY] * 8 + [VMEM],
        scratch_shapes=[
            pltpu.VMEM((4, total, width), BF16),
            pltpu.VMEM((4, parts * 4 * rank, width), BF16),
            pltpu.VMEM((4, total, width), BF16),
            pltpu.VMEM((total, width), F32),
            pltpu.VMEM((total, width), F32),
            pltpu.VMEM((4, parts * 4 * rank, width), BF16),
            pltpu.SemaphoreType.DMA((4, 4)),
            pltpu.SemaphoreType.DMA((4,)),
            pltpu.SemaphoreType.DMA((4, 3)),
        ],
        compiler_params=pltpu.CompilerParams(vmem_limit_bytes=56 * 2**20),
        name="attend",
    )(me, adapter, *units)


def move(x, axis, target):
    count = lax.axis_size(axis)
    return lax.ppermute(x, axis, [(i, target(i) % count) for i in range(count)])


def up(x):
    return move(x, "ctx", lambda i: i + 1)


def down_one(x):
    return move(x, "ctx", lambda i: i - 1)


def cross(x):
    return move(x, "ctx", lambda i: i + 2 if i % 2 == 0 else i - 2)


def cross_back(x):
    return move(x, "ctx", lambda i: i - 2 if i % 2 == 0 else i + 2)


def sibling(x):
    return move(x, "head", lambda i: i ^ 1)


def far_first(x):
    return lax.ppermute(x, "head", [(1, 3), (3, 1)])


def far_low(x, traded):
    low = lax.ppermute(x, "head", [(0, 2), (2, 0)])
    core = lax.rem(lax.axis_index("head"), 2)
    return jnp.where(core == 1, traded, low)


def far_second(x):
    return move(x, "head", lambda i: i ^ 2)


def head_sum(x):
    x = x + sibling(x)
    return x + move(x, "head", lambda i: i ^ 2)


def ctx_trade(x):
    return lax.all_to_all(x, "ctx", 0, 0, tiled=True)


def shards(
    inputs,
    queries,
    key_rows,
    value_rows,
    output_gradient,
    head_gradients,
    head_shift,
    down_qkv,
    up_qkv,
    output_down_adapter,
    up_out,
):
    rows_here, width = queries.shape
    heads_here = head_shift.shape[0]
    head_dim = width // heads_here
    place = lax.axis_index("ctx")
    column = lax.axis_index("head")
    me = jnp.stack([place, column]).astype(jnp.int32)
    rank, features = up_out.shape
    adapter = jnp.concatenate([up_qkv.reshape(3 * rank, width), output_down_adapter.T])
    own = (queries, key_rows, value_rows, head_gradients, adapter)
    with jax.named_scope("heads_in"):
        plan, case = make_plan(head_shift, me)
        sib = tuple(sibling(x) for x in own)
        case = case.reshape(())
        leaving = far_pack(plan, own, head_dim, 1)[0]
        far = far_first(leaving)
        inputs_late, gradient_late, _ = lax.optimization_barrier(
            (inputs, output_gradient, leaving)
        )

    with jax.named_scope("ranks_in"):
        output_part = jnp.einsum(
            "td,rd->rt", gradient_late, up_out, preferred_element_type=F32
        )
        input_part = jnp.einsum("td,kdr->krt", inputs_late, down_qkv, preferred_element_type=F32)
        rank_part = jnp.concatenate([input_part.reshape(3 * rank, rows_here), output_part])
        ranks = head_sum(rank_part).astype(BF16)

    with jax.named_scope("units"):

        def plain(far, sib, own, ranks, plan):
            return slot_pack(plan, own, sib, (far, far), ranks, head_dim)

        def two(far, sib, own, ranks, plan):
            traded = far_low(far_pack(plan, own, head_dim, 1)[0], far)
            return slot_pack(plan, own, sib, (traded, traded), ranks, head_dim)

        def more(far, sib, own, ranks, plan):
            first, second = far_pack(plan, own, head_dim, 2)
            traded = far_low(first, far), far_second(second)
            return slot_pack(plan, own, sib, traded, ranks, head_dim)

        slots = lax.switch(case, (plain, two, more), far, sib, own, ranks, plan)
        units = (cross(slots[3]), up(slots[1]), down_one(slots[2]), slots[0])
    results = attend(me, slots[4], units, rows_here, rank)

    with jax.named_scope("ranks_back"):
        pieces = (cross_back(results[7]), down_one(results[4]), up(results[6]), results[5])
        made = (results[8], sibling(results[8]), move(results[8], "head", lambda i: i ^ 2))
        pieces, made = lax.optimization_barrier((pieces, made))
        part = rank_add(pieces, rows_here, rank)
        part = part + sibling(part)
        other = move(part, "head", lambda i: i ^ 2)
        parts = fold(plan, me, part, other, inputs, output_gradient, made, rank)

    with jax.named_scope("heads_back"):
        crossed = cross_back(results[3])
        back = (results[1], down_one(results[0]), up(results[2]), crossed)

    with jax.named_scope("heads_home"):
        moved = {s: sibling(back[s]) for s in HOME_ORDER}
        back_sib = tuple(moved[s] for s in range(4))
        back_far = far_first(far_return_pack(plan, back, 1)[0])

        def plain_back():
            far = (back_far, back_far)
            return head_unpack(plan, back, back_sib, far, heads_here, rows_here)

        def two_back():
            traded = far_low(far_return_pack(plan, back, 1)[0], back_far)
            return head_unpack(plan, back, back_sib, (traded, traded), heads_here, rows_here)

        def more_back():
            first, second = far_return_pack(plan, back, 2)
            traded = far_low(first, back_far), far_second(second)
            return head_unpack(plan, back, back_sib, traded, heads_here, rows_here)

        projection_gradients = lax.switch(case, (plain_back, two_back, more_back))

    with jax.named_scope("token_sums"):
        scale = adapter_scale * (rows_here * lax.axis_size("ctx")) ** (-0.5)
        every = ctx_trade(sum_and_spread(ctx_trade(parts), scale))
        down, up_grad, out_down, out_up = unfold(every, rank, features)

    return (projection_gradients, down.transpose(0, 2, 1), up_grad, out_down.T, out_up)


def solution(mesh):
    placed = (
        P("ctx", "head"),
        P("ctx", "head"),
        P("ctx", "head"),
        P("ctx", "head"),
        P("ctx", "head"),
        P("ctx", "head"),
        P("head"),
        P(None, "head", None),
        P(None, None, "head"),
        P("head", None),
        P(None, "head"),
    )
    return jax.shard_map(
        shards,
        mesh=mesh,
        in_specs=placed,
        out_specs=(
            P(None, "ctx", "head"),
            P(None, "head", None),
            P(None, None, "head"),
            P("head", None),
            P(None, "head"),
        ),
        check_vma=False,
    )
```
